256 devices in a mesh: tm: 8 (over z), space: 32 (over x, y, core).
Axes of the slice: x: 4, y: 4, z: 8, core: 2. Of those that a mesh axis runs over, the one named last changes fastest.
Arguments:
- c_points: float32 [8, 160, 96, 256], P('tm', 'space'), may hold values from -6 to 6
- region: int32 [160, 96, 256], P('space'), may hold values from 0 to 2
- cond_scale: float32 [160, 96, 256], P('space'), may hold values from 0.5 to 2
- source: float32 [160, 96, 256], P('space'), may hold values from -6 to 6
- plan: int32 [32], P('tm'), may hold values from 0 to 3
Outputs:
- fine_states: float32 [32, 160, 96, 256], P('tm', 'space')
- corrected: float32 [8, 160, 96, 256], P('tm', 'space')
The draws below stay inside these ranges and needn't reach their ends.
All inputs are finite; a program needn't handle non-finite values.
Results may differ from the reference program's by a relative error of at most 0.00002.
Values sent between devices are 32-bit elements; how exact they have to be, the bound alone decides.
No kernel may reach another device: no remote copies, remote signals or barrier semaphores. Data moves between devices by JAX's collectives and lax.ppermute only.
A program may use at most 128 MiB of HBM per device.

```python
import math
import jax
import jax.numpy as jnp

NY = 96
NZ = 256
COARSEN = 4
SWEEPS = 4
NX = 160
COARSE = 8
STEPS = 32


def place_ends(values, own_key, least, top_value):
    shape = values.shape
    place = [jax.random.randint(jax.random.fold_in(own_key, axis), (), 0, shape[axis]) for axis in range(len(shape))]
    values = values.at[tuple(place)].set(least)
    longest = shape.index(max(shape))
    place[longest] = (place[longest] + 1) % shape[longest]
    return values.at[tuple(place)].set(top_value)


def shard_levels(own_key, shape, split, least, top_value):
    factor_of, own = 1.0, jax.random.fold_in(own_key, 6)
    for position, shards_of in split:
        steps = jnp.exp(jax.random.uniform(jax.random.fold_in(own, position), (shards_of,), jnp.float32, least / len(split), top_value / len(split)))
        factor_of = factor_of * jnp.repeat(steps, shape[position] // shards_of).reshape([-1 if axis == position else 1 for axis in range(len(shape))])
    return factor_of


def normal_values(stream_key, shape, scale, limit, cuts=(), kind=jnp.bfloat16):
    factor_of = shard_levels(stream_key, shape, cuts, -0.22, 0.18) if cuts else 1.0
    array = jax.random.normal(stream_key, shape, jnp.float32) * scale * factor_of
    return jnp.minimum(jnp.maximum(array, -limit), limit).astype(kind)


def setup_inputs(seed: int = 0) -> dict:
    keys = jax.random.split(jax.random.key(seed), 6)
    c_points = normal_values(keys[0], (COARSE, NX, NY, NZ), 1.0, 6.0, ((0, 8), (1, 32)), jnp.float32)
    region = place_ends(jax.random.randint(keys[1], (NX, NY, NZ), 0, 3), jax.random.fold_in(keys[1], 1), 0, 2).astype(jnp.int32)
    cond_scale = jnp.clip(jnp.exp(math.log(2.0) - 1.3862944 * jax.random.uniform(keys[2], (NX, NY, NZ), jnp.float32) ** shard_levels(keys[2], (NX, NY, NZ), ((0, 32),), -0.2, 0.2)), 0.5, 2.0)
    source = normal_values(keys[3], (NX, NY, NZ), 1.0, 6.0, ((0, 32),), jnp.float32)
    plan = place_ends(jax.random.randint(keys[4], (STEPS,), 0, 4), jax.random.fold_in(keys[4], 1), 0, 3).astype(jnp.int32)
    return {"c_points": c_points, "region": region, "cond_scale": cond_scale, "source": source, "plan": plan}


FINE_RATE = 4.0


def materials(region, cond_scale):
    cap = jnp.where(region == 0, 2.0, jnp.where(region == 1, 1.2, 1.6)).astype(jnp.float32)
    base = jnp.where(region == 0, 0.3, jnp.where(region == 1, 4.0, 2.5)).astype(jnp.float32)
    return cap, base * cond_scale


def face_set(cond):
    padded = jnp.pad(cond, 1)
    return (0.5 * (cond + padded[:-2, 1:-1, 1:-1]), 0.5 * (cond + padded[2:, 1:-1, 1:-1]),
            0.5 * (cond + padded[1:-1, :-2, 1:-1]), 0.5 * (cond + padded[1:-1, 2:, 1:-1]),
            0.5 * (cond + padded[1:-1, 1:-1, :-2]), 0.5 * (cond + padded[1:-1, 1:-1, 2:]))


def implicit(u_old, amp, rate, cap, source, faces):
    f0, f1, f2, f3, f4, f5 = faces
    diag = cap * rate + (((((f0 + f1) + f2) + f3) + f4) + f5)
    rhs = cap * rate * u_old + amp * source
    field = u_old
    for sweep in range(SWEEPS):
        up = jnp.pad(field, 1)
        total = rhs + f0 * up[:-2, 1:-1, 1:-1] + f1 * up[2:, 1:-1, 1:-1]
        total = total + f2 * up[1:-1, :-2, 1:-1] + f3 * up[1:-1, 2:, 1:-1]
        total = total + f4 * up[1:-1, 1:-1, :-2] + f5 * up[1:-1, 1:-1, 2:]
        field = total / diag
    return field


def reference(c_points, region, cond_scale, source, plan):
    cap, cond = materials(region, cond_scale)
    faces = face_set(cond)
    amps = plan.astype(jnp.float32) * 0.5
    amp_mean = jnp.mean(amps.reshape(COARSE, COARSEN), axis=1)
    coarse_rate = FINE_RATE / COARSEN
    fine = []
    tau = []
    for k in range(COARSE):
        field = c_points[k]
        for j in range(COARSEN):
            field = implicit(field, amps[k * COARSEN + j], FINE_RATE, cap, source, faces)
            fine.append(field)
        tau.append(field - implicit(c_points[k], amp_mean[k], coarse_rate, cap, source, faces))
    state = c_points[0]
    result = []
    for k in range(COARSE):
        state = implicit(state, amp_mean[k], coarse_rate, cap, source, faces) + tau[k]
        result.append(state)
    return jnp.stack(fine), jnp.stack(result)
```

```python
import functools
import jax
import jax.numpy as jnp
from jax import lax
from jax.experimental import pallas as pl
from jax.experimental.pallas import tpu as pltpu
from jax.sharding import PartitionSpec as P

F32 = jnp.float32
VM = pl.BlockSpec(memory_space=pltpu.VMEM)
SM = pl.BlockSpec(memory_space=pltpu.SMEM)
NY, NZ = 96, 256
NL = 5
W = 4
EXT = NL + 2 * W
SLAB = 12
HR = 40
OWN = 16


def call(body, outs, ins, scratch=(), name=None, flops=0, limit=40):
    return pl.pallas_call(
        body,
        out_shape=[jax.ShapeDtypeStruct(s, F32) for s in outs],
        in_specs=ins,
        out_specs=[VM] * len(outs),
        scratch_shapes=list(scratch),
        compiler_params=pltpu.CompilerParams(vmem_limit_bytes=limit * 2**20),
        cost_estimate=pl.CostEstimate(flops=flops, bytes_accessed=4_000_000, transcendentals=0),
        name=name,
    )


def up_roll(x, axis):
    return pltpu.roll(x, x.shape[axis] - 1, axis)


def down_roll(x, axis):
    return pltpu.roll(x, 1, axis)


def sweep_layer(l, src, beta, fx, fy, fz, inv):
    w = src[l]
    a = fy[l]
    b = fz[l]
    total = beta[l] + fx[l] * src[l - 1] + fx[l + 1] * src[l + 1]
    total = total + a * down_roll(w, 0) + up_roll(a * w, 0)
    total = total + b * down_roll(w, 1) + up_roll(b * w, 1)
    return total * inv[l]


def sweeps(wa, wb, beta, fx, fy, fz, inv, finish):
    for n, (src, dst) in enumerate(((wa, wb), (wb, wa), (wa, wb))):
        def one(l, _):
            dst[l] = sweep_layer(l, src, beta, fx, fy, fz, inv)
            return 0
        lax.fori_loop(n + 1, EXT - 1 - n, one, 0)
    def last(l, _):
        finish(l, sweep_layer(l, wb, beta, fx, fy, fz, inv))
        return 0
    lax.fori_loop(W, W + NL, last, 0)


def place_halo(par, dst, on, off, first, count):
    @pl.when(par == 0)
    def _():
        dst[W - count:W] = off[first:first + count]
        dst[W + NL:W + NL + count] = on[first:first + count]

    @pl.when(par == 1)
    def _():
        dst[W - count:W] = on[first:first + count]
        dst[W + NL:W + NL + count] = off[first:first + count]


def give_edges(par, src, at, on, off, first, count):
    @pl.when(par == 0)
    def _():
        on[first:first + count] = src[at + NL - count:at + NL]
        off[first:first + count] = src[at:at + count]

    @pl.when(par == 1)
    def _():
        on[first:first + count] = src[at:at + count]
        off[first:first + count] = src[at + NL - count:at + NL]


def prep_body(ids, c, region, scale, source, cond, cap, on, off):
    par = ids[1] % 2
    r = region[...]
    cap[...] = jnp.where(r == 0, 2.0, jnp.where(r == 1, 1.2, 1.6)).astype(F32)
    cond[...] = jnp.where(r == 0, 0.3, jnp.where(r == 1, 4.0, 2.5)).astype(F32) * scale[...]
    give_edges(par, c, 0, on, off, 0, 4)
    give_edges(par, cond, 0, on, off, 4, 4)
    give_edges(par, cap, 0, on, off, 8, 3)
    give_edges(par, source, 0, on, off, 11, 3)


def first_body(ids, plan, c, cond, cap, source, on, off,
               u, fx, fy, fz, inv, capx, srcx, invc, son, soff,
               condx, wa, wb, beta):
    sp = ids[1]
    par = sp % 2
    condx[W:W + NL] = cond[...]
    capx[W:W + NL] = cap[...]
    srcx[W:W + NL] = source[...]
    wa[W:W + NL] = c[...]
    place_halo(par, wa, on, off, 0, 4)
    place_halo(par, condx, on, off, 4, 4)
    place_halo(par, capx, on, off, 8, 3)
    place_halo(par, srcx, on, off, 11, 3)
    zero = jnp.zeros((W, NY, NZ), F32)

    @pl.when(sp == 0)
    def _():
        condx[0:W] = zero

    @pl.when(sp == ids[2] - 1)
    def _():
        condx[W + NL:EXT] = zero

    rows = lax.broadcasted_iota(jnp.int32, (NY, NZ), 0)
    lanes = lax.broadcasted_iota(jnp.int32, (NY, NZ), 1)
    amp = plan[0].astype(F32) * 0.5

    def coef(l, _):
        k = condx[l]
        f0 = 0.5 * (k + condx[l - 1])
        f1 = 0.5 * (k + condx[l + 1])
        f2 = 0.5 * (k + jnp.where(rows == 0, 0.0, down_roll(k, 0)))
        f3 = 0.5 * (k + jnp.where(rows == NY - 1, 0.0, up_roll(k, 0)))
        f4 = 0.5 * (k + jnp.where(lanes == 0, 0.0, down_roll(k, 1)))
        f5 = 0.5 * (k + jnp.where(lanes == NZ - 1, 0.0, up_roll(k, 1)))
        total = ((((f0 + f1) + f2) + f3) + f4) + f5
        heat = capx[l]
        fx[l] = f0
        fy[l] = jnp.where(rows == 0, 0.0, f2)
        fz[l] = jnp.where(lanes == 0, 0.0, f4)
        inv[l] = 1.0 / (heat * 4.0 + total)
        invc[l] = 1.0 / (heat + total)
        beta[l] = heat * 4.0 * wa[l] + amp * srcx[l]
        return 0
    lax.fori_loop(1, EXT - 1, coef, 0)
    fx[EXT - 1] = 0.5 * (condx[EXT - 1] + condx[EXT - 2])

    @pl.when(sp == 0)
    def _():
        fx[W] = jnp.zeros((NY, NZ), F32)

    @pl.when(sp == ids[2] - 1)
    def _():
        fx[W + NL] = jnp.zeros((NY, NZ), F32)

    def finish(l, v):
        u[l - W] = v
    sweeps(wa, wb, beta, fx, fy, fz, inv, finish)
    give_edges(par, u, 0, son, soff, 0, 4)


def fine_body(j, ids, plan, u_old, fx, fy, fz, inv, capx, srcx, on, off, u, son, soff, wa, wb, beta):
    par = ids[1] % 2
    wa[W:W + NL] = u_old[...]
    place_halo(par, wa, on, off, 0, 4)
    amp = plan[j].astype(F32) * 0.5

    def rhs(l, _):
        beta[l] = capx[l] * 4.0 * wa[l] + amp * srcx[l]
        return 0
    lax.fori_loop(1, EXT - 1, rhs, 0)

    def finish(l, v):
        u[l - W] = v
    sweeps(wa, wb, beta, fx, fy, fz, inv, finish)
    give_edges(par, u, 0, son, soff, 0, 4)


def last_body(j, ids, plan, u_old, fx, fy, fz, inv, capx, srcx, on, off, c_next, u, give, wa, wb, beta):
    par = ids[1] % 2
    wa[W:W + NL] = u_old[...]
    place_halo(par, wa, on, off, 0, 4)
    amp = plan[j].astype(F32) * 0.5

    def rhs(l, _):
        beta[l] = capx[l] * 4.0 * wa[l] + amp * srcx[l]
        return 0
    lax.fori_loop(1, EXT - 1, rhs, 0)

    def finish(l, v):
        u[l - W] = v
    sweeps(wa, wb, beta, fx, fy, fz, inv, finish)
    for l in range(NL):
        d = u[l] - c_next[l]
        for t in range(8):
            part = d[t * SLAB:(t + 1) * SLAB]
            give[t, l * SLAB:(l + 1) * SLAB] = part[:, :128]
            give[t, 60 + l * SLAB:60 + (l + 1) * SLAB] = part[:, 128:]


def slab_body(ids, fx, fy, fz, invc, capx, out):
    shift = (16 + 128 - 12 * ids[0]) % 128
    spare = jnp.zeros((128 - NY, NZ), F32)
    for n, ref in enumerate((fx, fy, fz, invc, capx)):
        def one(l, _):
            v = jnp.concatenate([ref[l], spare], axis=0)
            out[n, l] = pltpu.roll(v, shift, 0)[:HR]
            return 0
        lax.fori_loop(1, EXT if n == 0 else EXT - 1, one, 0)


def unpack(chunk, l):
    return jnp.concatenate([chunk[l * SLAB:(l + 1) * SLAB], chunk[60 + l * SLAB:60 + (l + 1) * SLAB]], axis=1)


DEPTHS = ((1, 12, 0), (2, 8, 12), (3, 4, 20), (5, 4, 24), (7, 4, 28))


def ypay_body(got, fwd, bwd):
    for l in range(NL):
        for k, deep, at in DEPTHS:
            v = unpack(got[k - 1], l)
            fwd[l, at:at + deep] = v[SLAB - deep:]
            bwd[l, at:at + deep] = v[:deep]


def ymerge_body(ids, got, low, high, dx, on, off):
    dx[...] = jnp.zeros((7, NL, HR, NZ), F32)
    halo = {k: (deep, at) for k, deep, at in DEPTHS}
    for l in range(NL):
        for k in range(1, 8):
            dx[k - 1, l, OWN:OWN + SLAB] = unpack(got[k - 1], l)
            if k in halo:
                deep, at = halo[k]
                dx[k - 1, l, OWN - deep:OWN] = low[l, at:at + deep]
                dx[k - 1, l, OWN + SLAB:OWN + SLAB + deep] = high[l, at:at + deep]
    give_edges(ids[1] % 2, dx.at[0], 0, on, off, 0, 4)


def merge_body(ids, e, low, high, ex, on, off):
    ex[...] = e[...]
    ex[:, OWN - 8:OWN] = low[...]
    ex[:, OWN + SLAB:OWN + SLAB + 8] = high[...]
    give_edges(ids[1] % 2, ex, 0, on, off, 0, 4)


def stage_body(k, kind, ids, coef, e, on, off, *rest):
    par = ids[1] % 2
    if kind == "last":
        a, wa, wb, beta = rest
    else:
        dx, a, nxt, p, q, wa, wb, beta = rest
    wa[W:W + NL] = e[...]
    place_halo(par, wa, on, off, 0, 4)
    fx, fy, fz, inv, cap = (coef.at[n] for n in range(5))

    def rhs(l, _):
        beta[l] = cap[l] * wa[l]
        return 0
    lax.fori_loop(1, EXT - 1, rhs, 0)

    def finish(l, v):
        wa[l] = v
    sweeps(wa, wb, beta, fx, fy, fz, inv, finish)
    for l in range(NL):
        v = wa[W + l]
        part = v[OWN:OWN + SLAB]
        a[l * SLAB:(l + 1) * SLAB] = part[:, :128]
        a[60 + l * SLAB:60 + (l + 1) * SLAB] = part[:, 128:]
        if kind != "last":
            nxt[l] = v + dx[k, l]
    if kind == "x":
        give_edges(par, nxt, 0, p, q, 0, 4)
    if kind == "y":
        p[...] = nxt[:, OWN + SLAB - 8:OWN + SLAB]
        q[...] = nxt[:, OWN:OWN + 8]


def final_body(f, got, out):
    for l in range(NL):
        for t in range(8):
            out[l, t * SLAB:(t + 1) * SLAB] = f[l, t * SLAB:(t + 1) * SLAB] + unpack(got[t], l)


def swap_on(x):
    n = lax.axis_size("space")
    return lax.ppermute(x, "space", [(i, i ^ 1) for i in range(n)])


def swap_off(x):
    n = lax.axis_size("space")
    return lax.ppermute(x, "space", [(i, (i + 1) % n if i % 2 else (i - 1) % n) for i in range(n)])


def round_x(on, off):
    got_off = swap_off(off)
    return swap_on(on), got_off


def shift_tm(x, by):
    n = lax.axis_size("tm")
    return lax.ppermute(x, "tm", [(i, (i + by) % n) for i in range(n)])


def on_device(c_points, region, cond_scale, source, plan):
    c = c_points[0]
    ids = jnp.stack([lax.axis_index("tm"), lax.axis_index("space"), lax.axis_size("space")]).astype(jnp.int32)
    own, edge, ext = (NL, NY, NZ), (W, NY, NZ), (EXT, NY, NZ)
    work = [pltpu.VMEM(ext, F32)] * 3
    cond, cap, on, off = call(prep_body, [own, own, (14, NY, NZ), (14, NY, NZ)], [SM] + [VM] * 4, name="prep")(
        ids, c, region, cond_scale, source)
    on, off = round_x(on, off)
    c_next = shift_tm(c, -1)
    u, fx, fy, fz, inv, capx, srcx, invc, on, off = call(
        first_body, [own] + [ext] * 7 + [edge] * 2, [SM, SM] + [VM] * 6,
        [pltpu.VMEM(ext, F32)] * 4, name="fine0", flops=40_000_000)(ids, plan, c, cond, cap, source, on, off)
    (coef,) = call(slab_body, [(5, EXT, HR, NZ)], [SM] + [VM] * 5, name="slab")(ids, fx, fy, fz, invc, capx)
    fine = [u]
    for j in (1, 2):
        on, off = round_x(on, off)
        u, on, off = call(functools.partial(fine_body, j), [own, edge, edge], [SM, SM] + [VM] * 9, work,
                          name="fine", flops=30_000_000)(ids, plan, u, fx, fy, fz, inv, capx, srcx, on, off)
        fine.append(u)
    on, off = round_x(on, off)
    u, give = call(functools.partial(last_body, 3), [own, (8, 120, 128)], [SM, SM] + [VM] * 10, work,
                   name="fine3", flops=30_000_000)(ids, plan, u, fx, fy, fz, inv, capx, srcx, on, off, c_next)
    fine.append(u)
    got = lax.all_to_all(give, "tm", 0, 0, tiled=True)
    fwd, bwd = call(ypay_body, [(NL, 32, NZ)] * 2, [VM], name="ypay")(got)
    low, high = shift_tm(fwd, 1), shift_tm(bwd, -1)
    slab, side = (NL, HR, NZ), (W, HR, NZ)
    dx, on, off = call(ymerge_body, [(7,) + slab, side, side], [SM] + [VM] * 3, name="ymerge")(ids, got, low, high)
    e = dx[0]
    small = [pltpu.VMEM((EXT, HR, NZ), F32)] * 3
    parts = [jnp.zeros((120, 128), F32)]
    for k in range(1, 8):
        on, off = round_x(on, off)
        kind = "last" if k == 7 else "y" if k in (3, 5) else "x"
        body = functools.partial(stage_body, k, kind)
        if kind == "last":
            (a,) = call(body, [(120, 128)], [SM] + [VM] * 4, small, name="stage")(ids, coef, e, on, off)
        else:
            pay = (NL, 8, NZ) if kind == "y" else side
            a, e, p, q = call(body, [(120, 128), slab, pay, pay], [SM] + [VM] * 5, small, name="stage")(
                ids, coef, e, on, off, dx)
            if kind == "y":
                low, high = shift_tm(p, 1), shift_tm(q, -1)
                e, on, off = call(merge_body, [slab, side, side], [SM] + [VM] * 3, name="merge")(ids, e, low, high)
            else:
                on, off = p, q
        parts.append(a)
    back = lax.all_to_all(jnp.stack(parts), "tm", 0, 0, tiled=True)
    (corrected,) = call(final_body, [own], [VM] * 2, name="final")(u, back)
    return jnp.stack(fine), corrected[None]


def solution(mesh):
    in_specs = (
        P("tm", "space", None, None),
        P("space", None, None),
        P("space", None, None),
        P("space", None, None),
        P("tm"),
    )
    out_specs = (P("tm", "space", None, None), P("tm", "space", None, None))
    return jax.shard_map(
        on_device, mesh=mesh, in_specs=in_specs, out_specs=out_specs, check_vma=False
    )
```

```python
import functools
import jax
import jax.numpy as jnp
from jax import lax
from jax.experimental import pallas as pl
from jax.experimental.pallas import tpu as pltpu
from jax.sharding import PartitionSpec as P

F32 = jnp.float32
VM = pl.BlockSpec(memory_space=pltpu.VMEM)
SM = pl.BlockSpec(memory_space=pltpu.SMEM)
HB = pl.BlockSpec(memory_space=pltpu.MemorySpace.HBM)
NY, NZ = 96, 256
NL = 5
W = 4
EXT = NL + 2 * W
SLAB = 12
HR = 40
OWN = 16


def call(body, outs, ins, scratch=(), name=None, flops=0, limit=40):
    return pl.pallas_call(
        body,
        out_shape=[jax.ShapeDtypeStruct(s, F32) for s in outs],
        in_specs=ins,
        out_specs=[VM] * len(outs),
        scratch_shapes=list(scratch),
        compiler_params=pltpu.CompilerParams(vmem_limit_bytes=limit * 2**20),
        cost_estimate=pl.CostEstimate(flops=flops, bytes_accessed=4_000_000, transcendentals=0),
        name=name,
    )


def up_roll(x, axis):
    return pltpu.roll(x, x.shape[axis] - 1, axis)


def down_roll(x, axis):
    return pltpu.roll(x, 1, axis)


def sweep_layer(l, src, beta, fx, fy, fz, inv):
    w = src[l]
    a = fy(l)
    b = fz(l)
    total = beta[l] + fx(l) * src[l - 1] + fx(l + 1) * src[l + 1]
    total = total + a * down_roll(w, 0) + up_roll(a * w, 0)
    total = total + b * down_roll(w, 1) + up_roll(b * w, 1)
    return total * inv(l)


def sweeps(wa, wb, beta, coefs, finish):
    for n, (src, dst) in enumerate(((wa, wb), (wb, wa), (wa, wb), (wb, None))):
        for l in range(n + 1, EXT - 1 - n):
            v = sweep_layer(l, src, beta, *coefs)
            if dst is None:
                finish(l, v)
            else:
                dst[l] = v


def place_halo(par, dst, on, off, first, count):
    @pl.when(par == 0)
    def _():
        dst[W - count:W] = off[first:first + count]
        dst[W + NL:W + NL + count] = on[first:first + count]

    @pl.when(par == 1)
    def _():
        dst[W - count:W] = on[first:first + count]
        dst[W + NL:W + NL + count] = off[first:first + count]


def give_edges(par, src, on, off, first, count, lo=0, hi=None):
    hi = src.shape[1] if hi is None else hi

    @pl.when(par == 0)
    def _():
        on[first:first + count] = src[NL - count:NL, lo:hi]
        off[first:first + count] = src[0:count, lo:hi]

    @pl.when(par == 1)
    def _():
        on[first:first + count] = src[0:count, lo:hi]
        off[first:first + count] = src[NL - count:NL, lo:hi]


def run_copies(pairs, sems):
    copies = [pltpu.make_async_copy(src, dst, sems.at[n]) for n, (src, dst) in enumerate(pairs)]
    for copy in copies:
        copy.start()
    for copy in copies:
        copy.wait()


def prep_body(ids, region, scale, cond, cap, on, off, r, s, sems):
    run_copies([(region, r), (scale, s)], sems)
    par = ids[1] % 2
    for l in range(NL):
        kind = r[l]
        cap[l] = jnp.where(kind == 0, 2.0, jnp.where(kind == 1, 1.2, 1.6)).astype(F32)
        cond[l] = jnp.where(kind == 0, 0.3, jnp.where(kind == 1, 4.0, 2.5)).astype(F32) * s[l]
    give_edges(par, cond, on, off, 0, 4)
    give_edges(par, cap, on, off, 4, 3)


def state_body(ids, c, source, on, off, sems):
    par = ids[1] % 2
    run_copies([
        (c.at[pl.ds(1 - par, 4)], on.at[0:4]),
        (c.at[pl.ds(par, 4)], off.at[0:4]),
        (source.at[pl.ds(2 - 2 * par, 3)], on.at[4:7]),
        (source.at[pl.ds(2 * par, 3)], off.at[4:7]),
    ], sems)


def coef_body(ids, cond, cap, on, off, fx, fy, fz, inv, capx, invc, condx):
    sp = ids[1]
    par = sp % 2
    condx[W:W + NL] = cond[...]
    capx[W:W + NL] = cap[...]
    place_halo(par, condx, on, off, 0, 4)
    place_halo(par, capx, on, off, 4, 3)
    zero = jnp.zeros((W, NY, NZ), F32)

    @pl.when(sp == 0)
    def _():
        condx[0:W] = zero

    @pl.when(sp == ids[2] - 1)
    def _():
        condx[W + NL:EXT] = zero

    rows = lax.broadcasted_iota(jnp.int32, (NY, NZ), 0)
    lanes = lax.broadcasted_iota(jnp.int32, (NY, NZ), 1)
    for l in range(1, EXT - 1):
        k = condx[l]
        f0 = 0.5 * (k + condx[l - 1])
        f1 = 0.5 * (k + condx[l + 1])
        f2 = 0.5 * (k + jnp.where(rows == 0, 0.0, down_roll(k, 0)))
        f3 = 0.5 * (k + jnp.where(rows == NY - 1, 0.0, up_roll(k, 0)))
        f4 = 0.5 * (k + jnp.where(lanes == 0, 0.0, down_roll(k, 1)))
        f5 = 0.5 * (k + jnp.where(lanes == NZ - 1, 0.0, up_roll(k, 1)))
        total = ((((f0 + f1) + f2) + f3) + f4) + f5
        heat = capx[l]
        fx[l] = f0
        fy[l] = jnp.where(rows == 0, 0.0, f2)
        fz[l] = jnp.where(lanes == 0, 0.0, f4)
        inv[l] = 1.0 / (heat * 4.0 + total)
        invc[l] = 1.0 / (heat + total)
    fx[EXT - 1] = 0.5 * (condx[EXT - 1] + condx[EXT - 2])

    @pl.when(sp == 0)
    def _():
        fx[W] = jnp.zeros((NY, NZ), F32)

    @pl.when(sp == ids[2] - 1)
    def _():
        fx[W + NL] = jnp.zeros((NY, NZ), F32)


def whole(ref):
    return lambda l: ref[l]


def fine_step(amp, wa, wb, beta, fx, fy, fz, inv, capx, srcx, u):
    for l in range(1, EXT - 1):
        beta[l] = capx[l] * 4.0 * wa[l] + amp * srcx[l]

    def finish(l, v):
        u[l - W] = v
    sweeps(wa, wb, beta, [whole(fx), whole(fy), whole(fz), whole(inv)], finish)


def first_body(ids, plan, c, source, fx, fy, fz, inv, capx, on, off, u, srcx, son, soff, wa, wb, beta, sems):
    par = ids[1] % 2
    run_copies([(c, wa.at[W:W + NL]), (source, srcx.at[W:W + NL])], sems)
    place_halo(par, wa, on, off, 0, 4)
    place_halo(par, srcx, on, off, 4, 3)
    fine_step(plan[0].astype(F32) * 0.5, wa, wb, beta, fx, fy, fz, inv, capx, srcx, u)
    give_edges(par, u, son, soff, 0, 4)


def fine_body(j, ids, plan, u_old, fx, fy, fz, inv, capx, srcx, on, off, u, son, soff, wa, wb, beta):
    par = ids[1] % 2
    wa[W:W + NL] = u_old[...]
    place_halo(par, wa, on, off, 0, 4)
    fine_step(plan[j].astype(F32) * 0.5, wa, wb, beta, fx, fy, fz, inv, capx, srcx, u)
    give_edges(par, u, son, soff, 0, 4)


def last_body(j, ids, plan, u_old, fx, fy, fz, inv, capx, srcx, on, off, c_next, u, give, wa, wb, beta):
    par = ids[1] % 2
    wa[W:W + NL] = u_old[...]
    place_halo(par, wa, on, off, 0, 4)
    fine_step(plan[j].astype(F32) * 0.5, wa, wb, beta, fx, fy, fz, inv, capx, srcx, u)
    for l in range(NL):
        d = u[l] - c_next[l]
        for t in range(8):
            part = d[t * SLAB:(t + 1) * SLAB]
            give[t, l * SLAB:(l + 1) * SLAB] = part[:, :128]
            give[t, 60 + l * SLAB:60 + (l + 1) * SLAB] = part[:, 128:]


def slab_body(ids, fx, fy, fz, invc, capx, out):
    shift = (16 + 128 - 12 * ids[0]) % 128
    spare = jnp.zeros((128 - NY, NZ), F32)
    for n, ref in enumerate((fx, fy, fz, invc, capx)):
        for l in range(1, EXT if n == 0 else EXT - 1):
            v = jnp.concatenate([ref[l], spare], axis=0)
            out[n, l] = pltpu.roll(v, shift, 0)[:HR]


def unpack(chunk, l):
    return jnp.concatenate([chunk[l * SLAB:(l + 1) * SLAB], chunk[60 + l * SLAB:60 + (l + 1) * SLAB]], axis=1)


DEPTHS = ((1, 12, 0), (2, 8, 12), (3, 4, 20), (5, 4, 24), (7, 4, 28))


def ypay_body(got, fwd, bwd):
    for l in range(NL):
        for k, deep, at in DEPTHS:
            v = unpack(got[k - 1], l)
            fwd[l, at:at + deep] = v[SLAB - deep:]
            bwd[l, at:at + deep] = v[:deep]


def ymerge_body(ids, got, low, high, dx, on, off):
    dx[...] = jnp.zeros((7, NL, HR, NZ), F32)
    halo = {k: (deep, at) for k, deep, at in DEPTHS}
    for l in range(NL):
        for k in range(1, 8):
            dx[k - 1, l, OWN:OWN + SLAB] = unpack(got[k - 1], l)
            if k in halo:
                deep, at = halo[k]
                dx[k - 1, l, OWN - deep:OWN] = low[l, at:at + deep]
                dx[k - 1, l, OWN + SLAB:OWN + SLAB + deep] = high[l, at:at + deep]
    give_edges(ids[1] % 2, dx.at[0], on, off, 0, 4)


def merge_body(ids, e, low, high, ex, on, off):
    ex[...] = e[...]
    ex[:, OWN - 8:OWN] = low[...]
    ex[:, OWN + SLAB:OWN + SLAB + 8] = high[...]
    give_edges(ids[1] % 2, ex, on, off, 0, 4, *WINDOWS[4])


WINDOWS = {1: (0, 40), 2: (8, 40), 3: (8, 32), 4: (8, 40), 5: (8, 32), 6: (8, 40), 7: (8, 32)}


def stage_body(k, kind, ids, coef, e, on, off, *rest):
    par = ids[1] % 2
    lo, hi = WINDOWS[k]
    if kind == "last":
        a, wa, wb, beta = rest
    else:
        dx, a, nxt, p, q, wa, wb, beta = rest
    wa[W:W + NL] = e[:, lo:hi]
    place_halo(par, wa, on, off, 0, 4)
    fx, fy, fz, inv, cap = [functools.partial(lambda n, l: coef[n, l, lo:hi], n) for n in range(5)]
    for l in range(1, EXT - 1):
        beta[l] = cap(l) * wa[l]

    def finish(l, v):
        l = l - W
        part = v[OWN - lo:OWN - lo + SLAB]
        a[l * SLAB:(l + 1) * SLAB] = part[:, :128]
        a[60 + l * SLAB:60 + (l + 1) * SLAB] = part[:, 128:]
        if kind != "last":
            if lo > 0:
                nxt[l, :lo] = jnp.zeros((lo, NZ), F32)
            if hi < HR:
                nxt[l, hi:] = jnp.zeros((HR - hi, NZ), F32)
            nxt[l, lo:hi] = v + dx[k, l, lo:hi]
    sweeps(wa, wb, beta, [fx, fy, fz, inv], finish)
    if kind == "x":
        give_edges(par, nxt, p, q, 0, 4, *WINDOWS[k + 1])
    if kind == "y":
        p[...] = nxt[:, OWN + SLAB - 8:OWN + SLAB]
        q[...] = nxt[:, OWN:OWN + 8]


def final_body(f, got, out):
    for l in range(NL):
        for t in range(8):
            out[l, t * SLAB:(t + 1) * SLAB] = f[l, t * SLAB:(t + 1) * SLAB] + unpack(got[t], l)


def swap_on(x):
    n = lax.axis_size("space")
    return lax.ppermute(x, "space", [(i, i ^ 1) for i in range(n)])


def swap_off(x):
    n = lax.axis_size("space")
    return lax.ppermute(x, "space", [(i, (i + 1) % n if i % 2 else (i - 1) % n) for i in range(n)])


def round_x(on, off):
    got_off = swap_off(off)
    return swap_on(on), got_off


def shift_tm(x, by):
    n = lax.axis_size("tm")
    return lax.ppermute(x, "tm", [(i, (i + by) % n) for i in range(n)])


def on_device(c_points, region, cond_scale, source, plan):
    c = c_points[0]
    ids = jnp.stack([lax.axis_index("tm"), lax.axis_index("space"), lax.axis_size("space")]).astype(jnp.int32)
    own, edge, ext, pay = (NL, NY, NZ), (W, NY, NZ), (EXT, NY, NZ), (7, NY, NZ)
    work = [pltpu.VMEM(ext, F32)] * 3
    cond, cap, on, off = call(
        prep_body, [own, own, pay, pay], [SM, HB, HB],
        [pltpu.VMEM(own, jnp.int32), pltpu.VMEM(own, F32), pltpu.SemaphoreType.DMA((2,))], name="prep")(
        ids, region, cond_scale)
    mat_on, mat_off = round_x(on, off)
    on, off = call(state_body, [pay, pay], [SM, HB, HB], [pltpu.SemaphoreType.DMA((4,))], name="state")(ids, c, source)
    on, off = round_x(on, off)
    c_next = shift_tm(c, -1)
    fx, fy, fz, inv, capx, invc = call(
        coef_body, [ext] * 6, [SM] + [VM] * 4, [pltpu.VMEM(ext, F32)], name="coef", flops=10_000_000)(
        ids, cond, cap, mat_on, mat_off)
    (coef,) = call(slab_body, [(5, EXT, HR, NZ)], [SM] + [VM] * 5, name="slab")(ids, fx, fy, fz, invc, capx)
    u, srcx, on, off = call(
        first_body, [own, ext, edge, edge], [SM, SM, HB, HB] + [VM] * 7,
        work + [pltpu.SemaphoreType.DMA((2,))], name="fine0", flops=30_000_000)(
        ids, plan, c, source, fx, fy, fz, inv, capx, on, off)
    fine = [u]
    for j in (1, 2):
        on, off = round_x(on, off)
        u, on, off = call(functools.partial(fine_body, j), [own, edge, edge], [SM, SM] + [VM] * 9, work,
                          name="fine", flops=30_000_000)(ids, plan, u, fx, fy, fz, inv, capx, srcx, on, off)
        fine.append(u)
    on, off = round_x(on, off)
    u, give = call(functools.partial(last_body, 3), [own, (8, 120, 128)], [SM, SM] + [VM] * 10, work,
                   name="fine3", flops=30_000_000)(ids, plan, u, fx, fy, fz, inv, capx, srcx, on, off, c_next)
    fine.append(u)
    got = lax.all_to_all(give, "tm", 0, 0, tiled=True)
    fwd, bwd = call(ypay_body, [(NL, 32, NZ)] * 2, [VM], name="ypay")(got)
    low, high = shift_tm(fwd, 1), shift_tm(bwd, -1)
    slab, side = (NL, HR, NZ), (W, HR, NZ)
    dx, on, off = call(ymerge_body, [(7,) + slab, side, side], [SM] + [VM] * 3, name="ymerge")(ids, got, low, high)
    e = dx[0]
    parts = [jnp.zeros((120, 128), F32)]
    for k in range(1, 8):
        on, off = round_x(on, off)
        kind = "last" if k == 7 else "y" if k in (3, 5) else "x"
        body = functools.partial(stage_body, k, kind)
        lo, hi = WINDOWS[k]
        small = [pltpu.VMEM((EXT, hi - lo, NZ), F32)] * 3
        if kind == "last":
            (a,) = call(body, [(120, 128)], [SM] + [VM] * 4, small, name="stage")(ids, coef, e, on, off)
        else:
            lo, hi = WINDOWS[k + 1]
            side = (W, hi - lo, NZ)
            ends = (NL, 8, NZ) if kind == "y" else side
            a, e, p, q = call(body, [(120, 128), slab, ends, ends], [SM] + [VM] * 5, small, name="stage")(
                ids, coef, e, on, off, dx)
            if kind == "y":
                low, high = shift_tm(p, 1), shift_tm(q, -1)
                e, on, off = call(merge_body, [slab, side, side], [SM] + [VM] * 3, name="merge")(ids, e, low, high)
            else:
                on, off = p, q
        parts.append(a)
    back = lax.all_to_all(jnp.stack(parts), "tm", 0, 0, tiled=True)
    (corrected,) = call(final_body, [own], [VM] * 2, name="final")(u, back)
    return jnp.stack(fine), corrected[None]


def solution(mesh):
    in_specs = (
        P("tm", "space", None, None),
        P("space", None, None),
        P("space", None, None),
        P("space", None, None),
        P("tm"),
    )
    out_specs = (P("tm", "space", None, None), P("tm", "space", None, None))
    return jax.shard_map(
        on_device, mesh=mesh, in_specs=in_specs, out_specs=out_specs, check_vma=False
    )
```

```python
import functools
import jax
import jax.numpy as jnp
from jax import lax
from jax.experimental import pallas as pl
from jax.experimental.pallas import tpu as pltpu
from jax.sharding import PartitionSpec as P

F32 = jnp.float32
VM = pl.BlockSpec(memory_space=pltpu.VMEM)
SM = pl.BlockSpec(memory_space=pltpu.SMEM)
HB = pl.BlockSpec(memory_space=pltpu.MemorySpace.HBM)
NY, NZ = 96, 256
NL = 5
W = 4
EXT = NL + 2 * W
SLAB = 12
HR = 40
OWN = 16


def call(body, outs, ins, scratch=(), name=None, flops=0, limit=40):
    return pl.pallas_call(
        body,
        out_shape=[jax.ShapeDtypeStruct(s, F32) for s in outs],
        in_specs=ins,
        out_specs=[VM] * len(outs),
        scratch_shapes=list(scratch),
        compiler_params=pltpu.CompilerParams(vmem_limit_bytes=limit * 2**20),
        cost_estimate=pl.CostEstimate(flops=flops, bytes_accessed=4_000_000, transcendentals=0),
        name=name,
    )


def up_roll(x, axis):
    return pltpu.roll(x, x.shape[axis] - 1, axis)


def down_roll(x, axis):
    return pltpu.roll(x, 1, axis)


def sweep_layer(l, src, beta, fx, fy, fz, inv):
    w = src[l]
    a = fy(l)
    b = fz(l)
    total = beta[l] + fx(l) * src[l - 1] + fx(l + 1) * src[l + 1]
    total = total + a * down_roll(w, 0) + up_roll(a * w, 0)
    total = total + b * down_roll(w, 1) + up_roll(b * w, 1)
    return total * inv(l)


def sweeps(wa, wb, beta, coefs, finish):
    for n, (src, dst) in enumerate(((wa, wb), (wb, wa), (wa, wb), (wb, None))):
        for l in range(n + 1, EXT - 1 - n):
            v = sweep_layer(l, src, beta, *coefs)
            if dst is None:
                finish(l, v)
            else:
                dst[l] = v


def place_halo(par, dst, on, off, first, count):
    @pl.when(par == 0)
    def _():
        dst[W - count:W] = off[first:first + count]
        dst[W + NL:W + NL + count] = on[first:first + count]

    @pl.when(par == 1)
    def _():
        dst[W - count:W] = on[first:first + count]
        dst[W + NL:W + NL + count] = off[first:first + count]


def give_edges(par, src, on, off, first, count, lo=0, hi=None):
    hi = src.shape[1] if hi is None else hi

    @pl.when(par == 0)
    def _():
        on[first:first + count] = src[NL - count:NL, lo:hi]
        off[first:first + count] = src[0:count, lo:hi]

    @pl.when(par == 1)
    def _():
        on[first:first + count] = src[0:count, lo:hi]
        off[first:first + count] = src[NL - count:NL, lo:hi]


def run_copies(pairs, sems):
    copies = [pltpu.make_async_copy(src, dst, sems.at[n]) for n, (src, dst) in enumerate(pairs)]
    for copy in copies:
        copy.start()
    for copy in copies:
        copy.wait()


def prep_body(ids, region, scale, cond, cap, on, off, r, s, sems):
    run_copies([(region, r), (scale, s)], sems)
    par = ids[1] % 2
    for l in range(NL):
        kind = r[l]
        cap[l] = jnp.where(kind == 0, 2.0, jnp.where(kind == 1, 1.2, 1.6)).astype(F32)
        cond[l] = jnp.where(kind == 0, 0.3, jnp.where(kind == 1, 4.0, 2.5)).astype(F32) * s[l]
    give_edges(par, cond, on, off, 0, 4)
    give_edges(par, cap, on, off, 4, 3)


def state_body(ids, c, source, on, off, sems):
    par = ids[1] % 2
    run_copies([
        (c.at[pl.ds(1 - par, 4)], on.at[0:4]),
        (c.at[pl.ds(par, 4)], off.at[0:4]),
        (source.at[pl.ds(2 - 2 * par, 3)], on.at[4:7]),
        (source.at[pl.ds(2 * par, 3)], off.at[4:7]),
    ], sems)


def coef_body(ids, cond, cap, on, off, fx, fy, fz, inv, capx, invc, condx):
    sp = ids[1]
    par = sp % 2
    condx[W:W + NL] = cond[...]
    capx[W:W + NL] = cap[...]
    place_halo(par, condx, on, off, 0, 4)
    place_halo(par, capx, on, off, 4, 3)
    zero = jnp.zeros((W, NY, NZ), F32)

    @pl.when(sp == 0)
    def _():
        condx[0:W] = zero

    @pl.when(sp == ids[2] - 1)
    def _():
        condx[W + NL:EXT] = zero

    rows = lax.broadcasted_iota(jnp.int32, (NY, NZ), 0)
    lanes = lax.broadcasted_iota(jnp.int32, (NY, NZ), 1)
    for l in range(1, EXT - 1):
        k = condx[l]
        f0 = 0.5 * (k + condx[l - 1])
        f1 = 0.5 * (k + condx[l + 1])
        f2 = 0.5 * (k + jnp.where(rows == 0, 0.0, down_roll(k, 0)))
        f3 = 0.5 * (k + jnp.where(rows == NY - 1, 0.0, up_roll(k, 0)))
        f4 = 0.5 * (k + jnp.where(lanes == 0, 0.0, down_roll(k, 1)))
        f5 = 0.5 * (k + jnp.where(lanes == NZ - 1, 0.0, up_roll(k, 1)))
        total = ((((f0 + f1) + f2) + f3) + f4) + f5
        heat = capx[l]
        fx[l] = f0
        fy[l] = jnp.where(rows == 0, 0.0, f2)
        fz[l] = jnp.where(lanes == 0, 0.0, f4)
        inv[l] = 1.0 / (heat * 4.0 + total)
        invc[l] = 1.0 / (heat + total)
    fx[EXT - 1] = 0.5 * (condx[EXT - 1] + condx[EXT - 2])

    @pl.when(sp == 0)
    def _():
        fx[W] = jnp.zeros((NY, NZ), F32)

    @pl.when(sp == ids[2] - 1)
    def _():
        fx[W + NL] = jnp.zeros((NY, NZ), F32)


def whole(ref):
    return lambda l: ref[l]


def fine_step(amp, wa, wb, beta, fx, fy, fz, inv, capx, srcx, u):
    for l in range(1, EXT - 1):
        beta[l] = capx[l] * 4.0 * wa[l] + amp * srcx[l]

    def finish(l, v):
        u[l - W] = v
    sweeps(wa, wb, beta, [whole(fx), whole(fy), whole(fz), whole(inv)], finish)


def first_body(ids, plan, c, source, fx, fy, fz, inv, capx, on, off, u, srcx, son, soff, wa, wb, beta, sems):
    par = ids[1] % 2
    run_copies([(c, wa.at[W:W + NL]), (source, srcx.at[W:W + NL])], sems)
    place_halo(par, wa, on, off, 0, 4)
    place_halo(par, srcx, on, off, 4, 3)
    fine_step(plan[0].astype(F32) * 0.5, wa, wb, beta, fx, fy, fz, inv, capx, srcx, u)
    give_edges(par, u, son, soff, 0, 4)


def fine_body(j, ids, plan, u_old, fx, fy, fz, inv, capx, srcx, on, off, u, son, soff, wa, wb, beta):
    par = ids[1] % 2
    wa[W:W + NL] = u_old[...]
    place_halo(par, wa, on, off, 0, 4)
    fine_step(plan[j].astype(F32) * 0.5, wa, wb, beta, fx, fy, fz, inv, capx, srcx, u)
    give_edges(par, u, son, soff, 0, 4)


def last_body(j, ids, plan, u_old, fx, fy, fz, inv, capx, srcx, on, off, c_next, u, give, wa, wb, beta):
    par = ids[1] % 2
    wa[W:W + NL] = u_old[...]
    place_halo(par, wa, on, off, 0, 4)
    fine_step(plan[j].astype(F32) * 0.5, wa, wb, beta, fx, fy, fz, inv, capx, srcx, u)
    for l in range(NL):
        d = u[l] - c_next[l]
        for t in range(8):
            part = d[t * SLAB:(t + 1) * SLAB]
            give[t, l * SLAB:(l + 1) * SLAB] = part[:, :128]
            give[t, 60 + l * SLAB:60 + (l + 1) * SLAB] = part[:, 128:]


def slab_body(ids, fx, fy, fz, invc, capx, out):
    shift = (16 + 128 - 12 * ids[0]) % 128
    spare = jnp.zeros((128 - NY, NZ), F32)
    for n, ref in enumerate((fx, fy, fz, invc, capx)):
        for l in range(1, EXT if n == 0 else EXT - 1):
            v = jnp.concatenate([ref[l], spare], axis=0)
            out[n, l] = pltpu.roll(v, shift, 0)[:HR]


def unpack(chunk, l):
    return jnp.concatenate([chunk[l * SLAB:(l + 1) * SLAB], chunk[60 + l * SLAB:60 + (l + 1) * SLAB]], axis=1)


DEPTHS = ((1, 12, 0), (2, 8, 12), (3, 4, 20), (5, 4, 24), (7, 4, 28))


def ypay_body(got, fwd, bwd):
    for l in range(NL):
        for k, deep, at in DEPTHS:
            v = unpack(got[k - 1], l)
            fwd[l, at:at + deep] = v[SLAB - deep:]
            bwd[l, at:at + deep] = v[:deep]


def ymerge_body(ids, got, low, high, dx, on, off):
    dx[...] = jnp.zeros((7, NL, HR, NZ), F32)
    halo = {k: (deep, at) for k, deep, at in DEPTHS}
    for l in range(NL):
        for k in range(1, 8):
            dx[k - 1, l, OWN:OWN + SLAB] = unpack(got[k - 1], l)
            if k in halo:
                deep, at = halo[k]
                dx[k - 1, l, OWN - deep:OWN] = low[l, at:at + deep]
                dx[k - 1, l, OWN + SLAB:OWN + SLAB + deep] = high[l, at:at + deep]
    give_edges(ids[1] % 2, dx.at[0], on, off, 0, 4)


def merge_body(ids, e, low, high, ex, on, off):
    ex[...] = e[...]
    ex[:, OWN - 8:OWN] = low[...]
    ex[:, OWN + SLAB:OWN + SLAB + 8] = high[...]
    give_edges(ids[1] % 2, ex, on, off, 0, 4, *WINDOWS[4])


WINDOWS = {1: (0, 40), 2: (8, 40), 3: (8, 32), 4: (8, 40), 5: (8, 32), 6: (8, 40), 7: (8, 32)}


def stage_body(k, kind, ids, coef, e, on, off, *rest):
    par = ids[1] % 2
    lo, hi = WINDOWS[k]
    if kind == "last":
        a, wa, wb, beta = rest
    else:
        dx, a, nxt, p, q, wa, wb, beta = rest
    wa[W:W + NL] = e[:, lo:hi]
    place_halo(par, wa, on, off, 0, 4)
    fx, fy, fz, inv, cap = [functools.partial(lambda n, l: coef[n, l, lo:hi], n) for n in range(5)]
    for l in range(1, EXT - 1):
        beta[l] = cap(l) * wa[l]

    def finish(l, v):
        l = l - W
        part = v[OWN - lo:OWN - lo + SLAB]
        a[l * SLAB:(l + 1) * SLAB] = part[:, :128]
        a[60 + l * SLAB:60 + (l + 1) * SLAB] = part[:, 128:]
        if kind != "last":
            if lo > 0:
                nxt[l, :lo] = jnp.zeros((lo, NZ), F32)
            if hi < HR:
                nxt[l, hi:] = jnp.zeros((HR - hi, NZ), F32)
            nxt[l, lo:hi] = v + dx[k, l, lo:hi]
    sweeps(wa, wb, beta, [fx, fy, fz, inv], finish)
    if kind == "x":
        give_edges(par, nxt, p, q, 0, 4, *WINDOWS[k + 1])
    if kind == "y":
        p[...] = nxt[:, OWN + SLAB - 8:OWN + SLAB]
        q[...] = nxt[:, OWN:OWN + 8]


def final_body(f, got, out):
    for l in range(NL):
        for t in range(8):
            out[l, t * SLAB:(t + 1) * SLAB] = f[l, t * SLAB:(t + 1) * SLAB] + unpack(got[t], l)


def swap_on(x):
    n = lax.axis_size("space")
    return lax.ppermute(x, "space", [(i, i ^ 1) for i in range(n)])


def swap_off(x):
    n, groups = lax.axis_size("space"), lax.axis_size("tm")
    pairs = []
    for t in range(groups):
        for i in range(n):
            if i in (0, n - 1):
                pairs.append((t * n + i, (t ^ 1) * n + i))
            else:
                pairs.append((t * n + i, t * n + (i + 1 if i % 2 else i - 1)))
    return lax.ppermute(x, ("tm", "space"), pairs)


def round_x(on, off):
    got_off = swap_off(off)
    return swap_on(on), got_off


def shift_tm(x, by):
    n = lax.axis_size("tm")
    return lax.ppermute(x, "tm", [(i, (i + by) % n) for i in range(n)])


def on_device(c_points, region, cond_scale, source, plan):
    c = c_points[0]
    ids = jnp.stack([lax.axis_index("tm"), lax.axis_index("space"), lax.axis_size("space")]).astype(jnp.int32)
    own, edge, ext, pay = (NL, NY, NZ), (W, NY, NZ), (EXT, NY, NZ), (7, NY, NZ)
    work = [pltpu.VMEM(ext, F32)] * 3
    cond, cap, on, off = call(
        prep_body, [own, own, pay, pay], [SM, HB, HB],
        [pltpu.VMEM(own, jnp.int32), pltpu.VMEM(own, F32), pltpu.SemaphoreType.DMA((2,))], name="prep")(
        ids, region, cond_scale)
    mat_on, mat_off = round_x(on, off)
    on, off = call(state_body, [pay, pay], [SM, HB, HB], [pltpu.SemaphoreType.DMA((4,))], name="state")(ids, c, source)
    on, off = round_x(on, off)
    c_next = shift_tm(c, -1)
    fx, fy, fz, inv, capx, invc = call(
        coef_body, [ext] * 6, [SM] + [VM] * 4, [pltpu.VMEM(ext, F32)], name="coef", flops=10_000_000)(
        ids, cond, cap, mat_on, mat_off)
    (coef,) = call(slab_body, [(5, EXT, HR, NZ)], [SM] + [VM] * 5, name="slab")(ids, fx, fy, fz, invc, capx)
    u, srcx, on, off = call(
        first_body, [own, ext, edge, edge], [SM, SM, HB, HB] + [VM] * 7,
        work + [pltpu.SemaphoreType.DMA((2,))], name="fine0", flops=30_000_000)(
        ids, plan, c, source, fx, fy, fz, inv, capx, on, off)
    fine = [u]
    for j in (1, 2):
        on, off = round_x(on, off)
        u, on, off = call(functools.partial(fine_body, j), [own, edge, edge], [SM, SM] + [VM] * 9, work,
                          name="fine", flops=30_000_000)(ids, plan, u, fx, fy, fz, inv, capx, srcx, on, off)
        fine.append(u)
    on, off = round_x(on, off)
    u, give = call(functools.partial(last_body, 3), [own, (8, 120, 128)], [SM, SM] + [VM] * 10, work,
                   name="fine3", flops=30_000_000)(ids, plan, u, fx, fy, fz, inv, capx, srcx, on, off, c_next)
    fine.append(u)
    got = lax.all_to_all(give, "tm", 0, 0, tiled=True)
    fwd, bwd = call(ypay_body, [(NL, 32, NZ)] * 2, [VM], name="ypay")(got)
    low, high = shift_tm(fwd, 1), shift_tm(bwd, -1)
    slab, side = (NL, HR, NZ), (W, HR, NZ)
    dx, on, off = call(ymerge_body, [(7,) + slab, side, side], [SM] + [VM] * 3, name="ymerge")(ids, got, low, high)
    e = dx[0]
    parts = [jnp.zeros((120, 128), F32)]
    for k in range(1, 8):
        on, off = round_x(on, off)
        kind = "last" if k == 7 else "y" if k in (3, 5) else "x"
        body = functools.partial(stage_body, k, kind)
        lo, hi = WINDOWS[k]
        small = [pltpu.VMEM((EXT, hi - lo, NZ), F32)] * 3
        if kind == "last":
            (a,) = call(body, [(120, 128)], [SM] + [VM] * 4, small, name="stage")(ids, coef, e, on, off)
        else:
            lo, hi = WINDOWS[k + 1]
            side = (W, hi - lo, NZ)
            ends = (NL, 8, NZ) if kind == "y" else side
            a, e, p, q = call(body, [(120, 128), slab, ends, ends], [SM] + [VM] * 5, small, name="stage")(
                ids, coef, e, on, off, dx)
            if kind == "y":
                low, high = shift_tm(p, 1), shift_tm(q, -1)
                e, on, off = call(merge_body, [slab, side, side], [SM] + [VM] * 3, name="merge")(ids, e, low, high)
            else:
                on, off = p, q
        parts.append(a)
    back = lax.all_to_all(jnp.stack(parts), "tm", 0, 0, tiled=True)
    (corrected,) = call(final_body, [own], [VM] * 2, name="final")(u, back)
    return jnp.stack(fine), corrected[None]


def solution(mesh):
    in_specs = (
        P("tm", "space", None, None),
        P("space", None, None),
        P("space", None, None),
        P("space", None, None),
        P("tm"),
    )
    out_specs = (P("tm", "space", None, None), P("tm", "space", None, None))
    return jax.shard_map(
        on_device, mesh=mesh, in_specs=in_specs, out_specs=out_specs, check_vma=False
    )
```

```python
import functools
import jax
import jax.numpy as jnp
from jax import lax
from jax.experimental import pallas as pl
from jax.experimental.pallas import tpu as pltpu
from jax.sharding import PartitionSpec as P

F32 = jnp.float32
VM = pl.BlockSpec(memory_space=pltpu.VMEM)
SM = pl.BlockSpec(memory_space=pltpu.SMEM)
HB = pl.BlockSpec(memory_space=pltpu.MemorySpace.HBM)
NY, NZ = 96, 256
NL = 5
W = 4
SWEEPS = 4
EXT = NL + 2 * W
SLAB = 12
HR = 40
OWN = 16


def call(body, outs, ins, scratch=(), name=None, flops=0, limit=40):
    return pl.pallas_call(
        body,
        out_shape=[jax.ShapeDtypeStruct(s, F32) for s in outs],
        in_specs=ins,
        out_specs=[VM] * len(outs),
        scratch_shapes=list(scratch),
        compiler_params=pltpu.CompilerParams(vmem_limit_bytes=limit * 2**20),
        cost_estimate=pl.CostEstimate(flops=flops, bytes_accessed=4_000_000, transcendentals=0),
        name=name,
    )


def up_roll(x, axis):
    return pltpu.roll(x, x.shape[axis] - 1, axis)


def down_roll(x, axis):
    return pltpu.roll(x, 1, axis)


def place_halo(par, dst, on, off, first, count):
    @pl.when(par == 0)
    def _():
        dst[W - count:W] = off[first:first + count]
        dst[W + NL:W + NL + count] = on[first:first + count]

    @pl.when(par == 1)
    def _():
        dst[W - count:W] = on[first:first + count]
        dst[W + NL:W + NL + count] = off[first:first + count]


def give_edges(par, src, on, off, first, count, lo=0, hi=None):
    hi = src.shape[1] if hi is None else hi

    @pl.when(par == 0)
    def _():
        on[first:first + count] = src[NL - count:NL, lo:hi]
        off[first:first + count] = src[0:count, lo:hi]

    @pl.when(par == 1)
    def _():
        on[first:first + count] = src[0:count, lo:hi]
        off[first:first + count] = src[NL - count:NL, lo:hi]


def run_copies(pairs, sems):
    copies = [pltpu.make_async_copy(src, dst, sems.at[n]) for n, (src, dst) in enumerate(pairs)]
    for copy in copies:
        copy.start()
    for copy in copies:
        copy.wait()


def prep_body(ids, region, scale, cond, cap, on, off, r, s, sems):
    run_copies([(region, r), (scale, s)], sems)
    par = ids[1] % 2
    for l in range(NL):
        kind = r[l]
        cap[l] = jnp.where(kind == 0, 2.0, jnp.where(kind == 1, 1.2, 1.6)).astype(F32)
        cond[l] = jnp.where(kind == 0, 0.3, jnp.where(kind == 1, 4.0, 2.5)).astype(F32) * s[l]
    give_edges(par, cond, on, off, 0, 4)
    give_edges(par, cap, on, off, 4, 3)


def state_body(ids, c, source, on, off, sems):
    par = ids[1] % 2
    run_copies([
        (c.at[pl.ds(1 - par, 4)], on.at[0:4]),
        (c.at[pl.ds(par, 4)], off.at[0:4]),
        (source.at[pl.ds(2 - 2 * par, 3)], on.at[4:7]),
        (source.at[pl.ds(2 * par, 3)], off.at[4:7]),
    ], sems)


def coef_body(ids, cond, cap, on, off, fx, fy, fz, inv, capx, slabs, invc, condx):
    sp = ids[1]
    par = sp % 2
    condx[W:W + NL] = cond[...]
    capx[W:W + NL] = cap[...]
    place_halo(par, condx, on, off, 0, 4)
    place_halo(par, capx, on, off, 4, 3)
    zero = jnp.zeros((W, NY, NZ), F32)

    @pl.when(sp == 0)
    def _():
        condx[0:W] = zero

    @pl.when(sp == ids[2] - 1)
    def _():
        condx[W + NL:EXT] = zero

    rows = lax.broadcasted_iota(jnp.int32, (NY, NZ), 0)
    lanes = lax.broadcasted_iota(jnp.int32, (NY, NZ), 1)
    for l in range(1, EXT - 1):
        k = condx[l]
        f0 = 0.5 * (k + condx[l - 1])
        f1 = 0.5 * (k + condx[l + 1])
        f2 = 0.5 * (k + jnp.where(rows == 0, 0.0, down_roll(k, 0)))
        f3 = 0.5 * (k + jnp.where(rows == NY - 1, 0.0, up_roll(k, 0)))
        f4 = 0.5 * (k + jnp.where(lanes == 0, 0.0, down_roll(k, 1)))
        f5 = 0.5 * (k + jnp.where(lanes == NZ - 1, 0.0, up_roll(k, 1)))
        total = ((((f0 + f1) + f2) + f3) + f4) + f5
        heat = capx[l]
        fx[l] = f0
        fy[l] = jnp.where(rows == 0, 0.0, f2)
        fz[l] = jnp.where(lanes == 0, 0.0, f4)
        inv[l] = 1.0 / (heat * 4.0 + total)
        invc[l] = 1.0 / (heat + total)
    fx[EXT - 1] = 0.5 * (condx[EXT - 1] + condx[EXT - 2])

    @pl.when(sp == 0)
    def _():
        fx[W] = jnp.zeros((NY, NZ), F32)

    @pl.when(sp == ids[2] - 1)
    def _():
        fx[W + NL] = jnp.zeros((NY, NZ), F32)

    shift = (16 + 128 - 12 * ids[0]) % 128
    spare = jnp.zeros((128 - NY, NZ), F32)
    for n, ref in enumerate((fx, fy, fz, invc, capx)):
        for l in range(1, EXT if n == 0 else EXT - 1):
            v = jnp.concatenate([ref[l], spare], axis=0)
            slabs[n, l] = pltpu.roll(v, shift, 0)[:HR]


EARLY = (((5, 11), (6, 10), (7, 9), (8, 8)), ((1, 7), (2, 6), (3, 5), (4, 4)))
LATE = (((1, 4), (2, 5), (3, 6), (4, 7)), ((8, 11), (7, 10), (6, 9), (5, 8)))


def fine_part(par, late, amp, u_old, got, source, src_got, fx, fy, fz, inv, capx, early, mine, store):
    spans = (LATE if late else EARLY)[par]
    high = (par == 0) != late
    start = W + NL if high else 0

    def has(n, l):
        return spans[n][0] <= l <= spans[n][1]

    def start_value(l):
        return u_old[l - W] if W <= l < W + NL else got[l - start]

    def heat(l):
        return source[l - W] if W <= l < W + NL else src_got[4 + l - (start if high else 1)]

    def value(n, l):
        if n == 0:
            return start_value(l)
        return (mine if has(n - 1, l) else early)[n][l]

    for n in range(SWEEPS):
        for l in range(spans[n][0], spans[n][1] + 1):
            if n == 0:
                rhs = capx[l] * 4.0 * start_value(l) + amp * heat(l)
                mine[0][l] = rhs
            else:
                rhs = (mine if has(0, l) else early)[0][l]
            w = value(n, l)
            a = fy[l]
            b = fz[l]
            total = rhs + fx[l] * value(n, l - 1) + fx[l + 1] * value(n, l + 1)
            total = total + a * down_roll(w, 0) + up_roll(a * w, 0)
            total = total + b * down_roll(w, 1) + up_roll(b * w, 1)
            v = total * inv[l]
            if n == SWEEPS - 1:
                store(l, v)
            else:
                mine[n + 1][l] = v


def early_body(j, ids, plan, u_old, got, source, src_got, fx, fy, fz, inv, capx, beta, w1, w2, w3, last):
    amp = plan[j].astype(F32) * 0.5
    mine = (beta, w1, w2, w3)

    def store(l, v):
        last[...] = v
    for par in (0, 1):
        @pl.when(ids[1] % 2 == par)
        def _():
            fine_part(par, False, amp, u_old, got, source, src_got, fx, fy, fz, inv, capx, mine, mine, store)


def late_body(j, ids, plan, u_old, got, source, src_got, fx, fy, fz, inv, capx, beta, w1, w2, w3, last, *rest):
    amp = plan[j].astype(F32) * 0.5
    if j == 3:
        c_next, u, give, *mine = rest
    else:
        u, son, soff, *mine = rest

    def store(l, v):
        u[l - W] = v
    for par in (0, 1):
        @pl.when(ids[1] % 2 == par)
        def _():
            fine_part(par, True, amp, u_old, got, source, src_got, fx, fy, fz, inv, capx, (beta, w1, w2, w3), mine, store)
            u[NL - 1 if par == 0 else 0] = last[...]
    if j < 3:
        give_edges(ids[1] % 2, u, son, soff, 0, 4)
        return
    for l in range(NL):
        d = u[l] - c_next[l]
        for t in range(8):
            part = d[t * SLAB:(t + 1) * SLAB]
            give[t, l * SLAB:(l + 1) * SLAB] = part[:, :128]
            give[t, 60 + l * SLAB:60 + (l + 1) * SLAB] = part[:, 128:]


def unpack(chunk, l):
    return jnp.concatenate([chunk[l * SLAB:(l + 1) * SLAB], chunk[60 + l * SLAB:60 + (l + 1) * SLAB]], axis=1)


DEPTHS = ((1, 12, 0), (2, 8, 12), (3, 4, 20), (5, 4, 24), (7, 4, 28))


def ypay_body(got, fwd, bwd):
    for l in range(NL):
        for k, deep, at in DEPTHS:
            v = unpack(got[k - 1], l)
            fwd[l, at:at + deep] = v[SLAB - deep:]
            bwd[l, at:at + deep] = v[:deep]


def ymerge_body(ids, got, low, high, dx, on, off):
    dx[...] = jnp.zeros((7, NL, HR, NZ), F32)
    halo = {k: (deep, at) for k, deep, at in DEPTHS}
    for l in range(NL):
        for k in range(1, 8):
            dx[k - 1, l, OWN:OWN + SLAB] = unpack(got[k - 1], l)
            if k in halo:
                deep, at = halo[k]
                dx[k - 1, l, OWN - deep:OWN] = low[l, at:at + deep]
                dx[k - 1, l, OWN + SLAB:OWN + SLAB + deep] = high[l, at:at + deep]
    give_edges(ids[1] % 2, dx.at[0], on, off, 0, 4)


def merge_body(ids, e, low, high, ex, on, off):
    ex[...] = e[...]
    ex[:, OWN - 8:OWN] = low[...]
    ex[:, OWN + SLAB:OWN + SLAB + 8] = high[...]
    give_edges(ids[1] % 2, ex, on, off, 0, 4, *WINDOWS[4])


WINDOWS = {1: (0, 40), 2: (8, 40), 3: (8, 32), 4: (8, 40), 5: (8, 32), 6: (8, 40), 7: (8, 32)}


def stage_body(k, kind, ids, coef, e, on, off, *rest):
    par = ids[1] % 2
    lo, hi = WINDOWS[k]
    if kind == "last":
        a, wa, wb, beta = rest
    else:
        dx, a, nxt, p, q, wa, wb, beta = rest
    place_halo(par, wa, on, off, 0, 4)
    fx, fy, fz, inv, cap = [functools.partial(lambda n, l: coef[n, l, lo:hi], n) for n in range(5)]

    def start_value(l):
        return e[l - W, lo:hi] if W <= l < W + NL else wa[l]

    for n, (src, dst) in enumerate(((start_value, wb), (wb, wa), (wa, wb), (wb, None))):
        for l in range(n + 1, EXT - 1 - n):
            if n == 0:
                w, left, right = src(l), src(l - 1), src(l + 1)
                rhs = cap(l) * w
                beta[l] = rhs
            else:
                w, left, right = src[l], src[l - 1], src[l + 1]
                rhs = beta[l]
            f, g = fy(l), fz(l)
            total = rhs + fx(l) * left + fx(l + 1) * right
            total = total + f * down_roll(w, 0) + up_roll(f * w, 0)
            total = total + g * down_roll(w, 1) + up_roll(g * w, 1)
            v = total * inv(l)
            if dst is not None:
                dst[l] = v
                continue
            i = l - W
            part = v[OWN - lo:OWN - lo + SLAB]
            a[i * SLAB:(i + 1) * SLAB] = part[:, :128]
            a[60 + i * SLAB:60 + (i + 1) * SLAB] = part[:, 128:]
            if kind == "last":
                continue
            if kind == "y":
                nxt[i, :lo] = jnp.zeros((lo, NZ), F32)
                nxt[i, hi:] = jnp.zeros((HR - hi, NZ), F32)
            nxt[i, lo:hi] = v + dx[k, i, lo:hi]
    if kind == "x":
        give_edges(par, nxt, p, q, 0, 4, *WINDOWS[k + 1])
    if kind == "y":
        p[...] = nxt[:, OWN + SLAB - 8:OWN + SLAB]
        q[...] = nxt[:, OWN:OWN + 8]


def final_body(f, got, out):
    for l in range(NL):
        for t in range(8):
            out[l, t * SLAB:(t + 1) * SLAB] = f[l, t * SLAB:(t + 1) * SLAB] + unpack(got[t], l)


def swap_on(x):
    n = lax.axis_size("space")
    return lax.ppermute(x, "space", [(i, i ^ 1) for i in range(n)])


def swap_off(x):
    n, groups = lax.axis_size("space"), lax.axis_size("tm")
    pairs = []
    for t in range(groups):
        for i in range(n):
            if i in (0, n - 1):
                pairs.append((t * n + i, (t ^ 1) * n + i))
            else:
                pairs.append((t * n + i, t * n + (i + 1 if i % 2 else i - 1)))
    return lax.ppermute(x, ("tm", "space"), pairs)


def round_x(on, off):
    got_off = swap_off(off)
    return swap_on(on), got_off


def shift_tm(x, by):
    n = lax.axis_size("tm")
    return lax.ppermute(x, "tm", [(i, (i + by) % n) for i in range(n)])


def on_device(c_points, region, cond_scale, source, plan):
    c = c_points[0]
    ids = jnp.stack([lax.axis_index("tm"), lax.axis_index("space"), lax.axis_size("space")]).astype(jnp.int32)
    own, edge, ext, pay = (NL, NY, NZ), (W, NY, NZ), (EXT, NY, NZ), (7, NY, NZ)
    cond, cap, on, off = call(
        prep_body, [own, own, pay, pay], [SM, HB, HB],
        [pltpu.VMEM(own, jnp.int32), pltpu.VMEM(own, F32), pltpu.SemaphoreType.DMA((2,))], name="prep")(
        ids, region, cond_scale)
    mat_on, mat_off = round_x(on, off)
    on, off = call(state_body, [pay, pay], [SM, HB, HB], [pltpu.SemaphoreType.DMA((4,))], name="state")(ids, c, source)
    on, off = round_x(on, off)
    c_next = shift_tm(c, -1)
    fx, fy, fz, inv, capx, coef = call(
        coef_body, [ext] * 5 + [(5, EXT, HR, NZ)], [SM] + [VM] * 4, [pltpu.VMEM(ext, F32)] * 2, name="coef",
        flops=10_000_000)(ids, cond, cap, mat_on, mat_off)
    src_on, src_off = on, off
    u, fine = c, []
    for j in range(4):
        if j > 0:
            on, off = round_x(on, off)
        early = call(functools.partial(early_body, j), [ext] * 4 + [(NY, NZ)], [SM, SM] + [VM] * 9, name="early",
                     flops=15_000_000, limit=16)(ids, plan, u, on, source, src_on, fx, fy, fz, inv, capx)
        args = (ids, plan, u, off, source, src_off, fx, fy, fz, inv, capx, *early)
        if j < 3:
            u, on, off = call(functools.partial(late_body, j), [own, edge, edge], [SM, SM] + [VM] * 14,
                              [pltpu.VMEM(ext, F32)] * 4, name="late", flops=15_000_000, limit=16)(*args)
        else:
            u, give = call(functools.partial(late_body, j), [own, (8, 120, 128)], [SM, SM] + [VM] * 15,
                           [pltpu.VMEM(ext, F32)] * 4, name="late", flops=15_000_000, limit=16)(*args, c_next)
        fine.append(u)
    got = lax.all_to_all(give, "tm", 0, 0, tiled=True)
    fwd, bwd = call(ypay_body, [(NL, 32, NZ)] * 2, [VM], name="ypay")(got)
    low, high = shift_tm(fwd, 1), shift_tm(bwd, -1)
    slab, side = (NL, HR, NZ), (W, HR, NZ)
    dx, on, off = call(ymerge_body, [(7,) + slab, side, side], [SM] + [VM] * 3, name="ymerge")(ids, got, low, high)
    e = dx[0]
    parts = [jnp.zeros((120, 128), F32)]
    for k in range(1, 8):
        on, off = round_x(on, off)
        kind = "last" if k == 7 else "y" if k in (3, 5) else "x"
        body = functools.partial(stage_body, k, kind)
        lo, hi = WINDOWS[k]
        small = [pltpu.VMEM((EXT, hi - lo, NZ), F32)] * 3
        if kind == "last":
            (a,) = call(body, [(120, 128)], [SM] + [VM] * 4, small, name="stage")(ids, coef, e, on, off)
        else:
            lo, hi = WINDOWS[k + 1]
            side = (W, hi - lo, NZ)
            ends = (NL, 8, NZ) if kind == "y" else side
            a, e, p, q = call(body, [(120, 128), slab, ends, ends], [SM] + [VM] * 5, small, name="stage")(
                ids, coef, e, on, off, dx)
            if kind == "y":
                low, high = shift_tm(p, 1), shift_tm(q, -1)
                e, on, off = call(merge_body, [slab, side, side], [SM] + [VM] * 3, name="merge")(ids, e, low, high)
            else:
                on, off = p, q
        parts.append(a)
    back = lax.all_to_all(jnp.stack(parts), "tm", 0, 0, tiled=True)
    (corrected,) = call(final_body, [own], [VM] * 2, name="final")(u, back)
    return jnp.stack(fine), corrected[None]


def solution(mesh):
    in_specs = (
        P("tm", "space", None, None),
        P("space", None, None),
        P("space", None, None),
        P("space", None, None),
        P("tm"),
    )
    out_specs = (P("tm", "space", None, None), P("tm", "space", None, None))
    return jax.shard_map(
        on_device, mesh=mesh, in_specs=in_specs, out_specs=out_specs, check_vma=False
    )
```

```python
import functools
import jax
import jax.numpy as jnp
from jax import lax
from jax.experimental import pallas as pl
from jax.experimental.pallas import tpu as pltpu
from jax.sharding import PartitionSpec as P

F32 = jnp.float32
VM = pl.BlockSpec(memory_space=pltpu.VMEM)
SM = pl.BlockSpec(memory_space=pltpu.SMEM)
HB = pl.BlockSpec(memory_space=pltpu.MemorySpace.HBM)
NY, NZ = 96, 256
NL = 5
W = 4
SWEEPS = 4
EXT = NL + 2 * W
SLAB = 12
HR = 40
OWN = 16


def call(body, outs, ins, scratch=(), name=None, flops=0, limit=40):
    return pl.pallas_call(
        body,
        out_shape=[jax.ShapeDtypeStruct(s, F32) for s in outs],
        in_specs=ins,
        out_specs=[VM] * len(outs),
        scratch_shapes=list(scratch),
        compiler_params=pltpu.CompilerParams(vmem_limit_bytes=limit * 2**20),
        cost_estimate=pl.CostEstimate(flops=flops, bytes_accessed=4_000_000, transcendentals=0),
        name=name,
    )


def up_roll(x, axis):
    return pltpu.roll(x, x.shape[axis] - 1, axis)


def down_roll(x, axis):
    return pltpu.roll(x, 1, axis)


def place_halo(par, dst, on, off, first, count):
    @pl.when(par == 0)
    def _():
        dst[W - count:W] = off[first:first + count]
        dst[W + NL:W + NL + count] = on[first:first + count]

    @pl.when(par == 1)
    def _():
        dst[W - count:W] = on[first:first + count]
        dst[W + NL:W + NL + count] = off[first:first + count]


def give_edges(par, src, on, off, first, count, lo=0, hi=None):
    hi = src.shape[1] if hi is None else hi

    @pl.when(par == 0)
    def _():
        on[first:first + count] = src[NL - count:NL, lo:hi]
        off[first:first + count] = src[0:count, lo:hi]

    @pl.when(par == 1)
    def _():
        on[first:first + count] = src[0:count, lo:hi]
        off[first:first + count] = src[NL - count:NL, lo:hi]


def put_edge(par, on, off, i, v):
    low, high = (off, on) if par == 0 else (on, off)
    if i < W:
        low[i] = v
    if i >= NL - W:
        high[i - (NL - W)] = v


def prep_body(ids, region, scale, cond, cap, on, off):
    par = ids[1] % 2
    for l in range(NL):
        kind = region[l]
        cap[l] = jnp.where(kind == 0, 2.0, jnp.where(kind == 1, 1.2, 1.6)).astype(F32)
        cond[l] = jnp.where(kind == 0, 0.3, jnp.where(kind == 1, 4.0, 2.5)).astype(F32) * scale[l]
    give_edges(par, cond, on, off, 0, 4)
    give_edges(par, cap, on, off, 4, 3)


def state_body(ids, c, source, on, off, sems):
    par = ids[1] % 2
    copies = [pltpu.make_async_copy(src, dst, sems.at[n]) for n, (src, dst) in enumerate([
        (c.at[pl.ds(1 - par, 4)], on.at[0:4]),
        (c.at[pl.ds(par, 4)], off.at[0:4]),
        (source.at[pl.ds(2 - 2 * par, 3)], on.at[4:7]),
        (source.at[pl.ds(2 * par, 3)], off.at[4:7]),
    ])]
    for copy in copies:
        copy.start()
    for copy in copies:
        copy.wait()


def coef_body(ids, cond, cap, on, off, fx, fy, fz, inv, capx, slabs, invc, condx):
    sp = ids[1]
    par = sp % 2
    condx[W:W + NL] = cond[...]
    capx[W:W + NL] = cap[...]
    place_halo(par, condx, on, off, 0, 4)
    place_halo(par, capx, on, off, 4, 3)
    zero = jnp.zeros((W, NY, NZ), F32)

    @pl.when(sp == 0)
    def _():
        condx[0:W] = zero

    @pl.when(sp == ids[2] - 1)
    def _():
        condx[W + NL:EXT] = zero

    rows = lax.broadcasted_iota(jnp.int32, (NY, NZ), 0)
    lanes = lax.broadcasted_iota(jnp.int32, (NY, NZ), 1)
    for l in range(1, EXT - 1):
        k = condx[l]
        f0 = 0.5 * (k + condx[l - 1])
        f1 = 0.5 * (k + condx[l + 1])
        f2 = 0.5 * (k + jnp.where(rows == 0, 0.0, down_roll(k, 0)))
        f3 = 0.5 * (k + jnp.where(rows == NY - 1, 0.0, up_roll(k, 0)))
        f4 = 0.5 * (k + jnp.where(lanes == 0, 0.0, down_roll(k, 1)))
        f5 = 0.5 * (k + jnp.where(lanes == NZ - 1, 0.0, up_roll(k, 1)))
        total = ((((f0 + f1) + f2) + f3) + f4) + f5
        heat = capx[l]
        fx[l] = f0
        fy[l] = jnp.where(rows == 0, 0.0, f2)
        fz[l] = jnp.where(lanes == 0, 0.0, f4)
        inv[l] = 1.0 / (heat * 4.0 + total)
        invc[l] = 1.0 / (heat + total)
    fx[EXT - 1] = 0.5 * (condx[EXT - 1] + condx[EXT - 2])

    @pl.when(sp == 0)
    def _():
        fx[W] = jnp.zeros((NY, NZ), F32)

    @pl.when(sp == ids[2] - 1)
    def _():
        fx[W + NL] = jnp.zeros((NY, NZ), F32)

    shift = (16 + 128 - 12 * ids[0]) % 128
    spare = jnp.zeros((128 - NY, NZ), F32)
    for n, ref in enumerate((fx, fy, fz, invc, capx)):
        for l in range(1, EXT if n == 0 else EXT - 1):
            v = jnp.concatenate([ref[l], spare], axis=0)
            slabs[n, l] = pltpu.roll(v, shift, 0)[:HR]


EARLY = (((5, 11), (6, 10), (7, 9), (8, 8)), ((1, 7), (2, 6), (3, 5), (4, 4)))
LATE = (((1, 4), (2, 5), (3, 6), (4, 7)), ((8, 11), (7, 10), (6, 9), (5, 8)))


def fine_part(par, late, amp, u_old, got, source, src_got, fx, fy, fz, inv, capx, early, mine, store):
    spans = (LATE if late else EARLY)[par]
    high = (par == 0) != late
    start = W + NL if high else 0

    def has(n, l):
        return spans[n][0] <= l <= spans[n][1]

    def start_value(l):
        return u_old[l - W] if W <= l < W + NL else got[l - start]

    def heat(l):
        return source[l - W] if W <= l < W + NL else src_got[4 + l - (start if high else 1)]

    def value(n, l):
        if n == 0:
            return start_value(l)
        return (mine if has(n - 1, l) else early)[n][l]

    for n in range(SWEEPS):
        for l in range(spans[n][0], spans[n][1] + 1):
            if n == 0:
                rhs = capx[l] * 4.0 * start_value(l) + amp * heat(l)
                mine[0][l] = rhs
            else:
                rhs = (mine if has(0, l) else early)[0][l]
            w = value(n, l)
            a = fy[l]
            b = fz[l]
            total = rhs + fx[l] * value(n, l - 1) + fx[l + 1] * value(n, l + 1)
            total = total + a * down_roll(w, 0) + up_roll(a * w, 0)
            total = total + b * down_roll(w, 1) + up_roll(b * w, 1)
            v = total * inv[l]
            if n == SWEEPS - 1:
                store(l, v)
            else:
                mine[n + 1][l] = v


def early_body(j, ids, plan, u_old, got, source, src_got, fx, fy, fz, inv, capx, beta, w1, w2, w3, last):
    amp = plan[j].astype(F32) * 0.5
    mine = (beta, w1, w2, w3)

    def store(l, v):
        last[...] = v
    for par in (0, 1):
        @pl.when(ids[1] % 2 == par)
        def _():
            fine_part(par, False, amp, u_old, got, source, src_got, fx, fy, fz, inv, capx, mine, mine, store)


def late_body(j, ids, plan, u_old, got, source, src_got, fx, fy, fz, inv, capx, beta, w1, w2, w3, last, *rest):
    amp = plan[j].astype(F32) * 0.5
    if j == 3:
        c_next, u, give, *mine = rest
    else:
        u, son, soff, *mine = rest

    def store(par, l, v):
        u[l - W] = v
        if j < 3:
            put_edge(par, son, soff, l - W, v)
    for par in (0, 1):
        @pl.when(ids[1] % 2 == par)
        def _():
            fine_part(par, True, amp, u_old, got, source, src_got, fx, fy, fz, inv, capx, (beta, w1, w2, w3), mine,
                      functools.partial(store, par))
            store(par, W + NL - 1 if par == 0 else W, last[...])
    if j < 3:
        return
    for l in range(NL):
        d = u[l] - c_next[l]
        for t in range(8):
            part = d[t * SLAB:(t + 1) * SLAB]
            give[t, l * SLAB:(l + 1) * SLAB] = part[:, :128]
            give[t, 60 + l * SLAB:60 + (l + 1) * SLAB] = part[:, 128:]


def unpack(chunk, l):
    return jnp.concatenate([chunk[l * SLAB:(l + 1) * SLAB], chunk[60 + l * SLAB:60 + (l + 1) * SLAB]], axis=1)


DEPTHS = ((1, 12, 0), (2, 8, 12), (3, 4, 20), (5, 4, 24), (7, 4, 28))


def ypay_body(got, fwd, bwd):
    for l in range(NL):
        for k, deep, at in DEPTHS:
            v = unpack(got[k - 1], l)
            fwd[l, at:at + deep] = v[SLAB - deep:]
            bwd[l, at:at + deep] = v[:deep]


def ymerge_body(ids, got, low, high, dx, on, off):
    dx[...] = jnp.zeros((7, NL, HR, NZ), F32)
    halo = {k: (deep, at) for k, deep, at in DEPTHS}
    for l in range(NL):
        for k in range(1, 8):
            dx[k - 1, l, OWN:OWN + SLAB] = unpack(got[k - 1], l)
            if k in halo:
                deep, at = halo[k]
                dx[k - 1, l, OWN - deep:OWN] = low[l, at:at + deep]
                dx[k - 1, l, OWN + SLAB:OWN + SLAB + deep] = high[l, at:at + deep]
    give_edges(ids[1] % 2, dx.at[0], on, off, 0, 4)


def merge_body(ids, e, low, high, ex, on, off):
    ex[...] = e[...]
    ex[:, OWN - 8:OWN] = low[...]
    ex[:, OWN + SLAB:OWN + SLAB + 8] = high[...]
    give_edges(ids[1] % 2, ex, on, off, 0, 4, *WINDOWS[4])


WINDOWS = {1: (0, 40), 2: (8, 40), 3: (8, 32), 4: (8, 40), 5: (8, 32), 6: (8, 40), 7: (8, 32)}


def stage_body(k, kind, ids, *refs):
    for par in (0, 1):
        @pl.when(ids[1] % 2 == par)
        def _():
            stage_part(k, kind, par, *refs)


def stage_part(k, kind, par, coef, e, on, off, *rest):
    lo, hi = WINDOWS[k]
    if kind == "last":
        a, wa, wb, beta = rest
    else:
        dx, a, nxt, p, q, wa, wb, beta = rest
    low, high = (off, on) if par == 0 else (on, off)
    fx, fy, fz, inv, cap = [functools.partial(lambda n, l: coef[n, l, lo:hi], n) for n in range(5)]

    def start_value(l):
        if W <= l < W + NL:
            return e[l - W, lo:hi]
        return low[l] if l < W else high[l - W - NL]

    for n, (src, dst) in enumerate(((start_value, wb), (wb, wa), (wa, wb), (wb, None))):
        for l in range(n + 1, EXT - 1 - n):
            if n == 0:
                w, left, right = src(l), src(l - 1), src(l + 1)
                rhs = cap(l) * w
                beta[l] = rhs
            else:
                w, left, right = src[l], src[l - 1], src[l + 1]
                rhs = beta[l]
            f, g = fy(l), fz(l)
            total = rhs + fx(l) * left + fx(l + 1) * right
            total = total + f * down_roll(w, 0) + up_roll(f * w, 0)
            total = total + g * down_roll(w, 1) + up_roll(g * w, 1)
            v = total * inv(l)
            if dst is not None:
                dst[l] = v
                continue
            i = l - W
            a[i] = v[OWN - lo:OWN - lo + 16]
            if kind == "last":
                continue
            v = v + dx[k, i, lo:hi]
            nxt[i, lo:hi] = v
            if kind == "x":
                at, end = WINDOWS[k + 1]
                put_edge(par, p, q, i, v[at - lo:end - lo])
            else:
                nxt[i, :lo] = jnp.zeros((lo, NZ), F32)
                nxt[i, hi:] = jnp.zeros((HR - hi, NZ), F32)
                p[i] = v[OWN + SLAB - 8 - lo:OWN + SLAB - lo]
                q[i] = v[OWN - lo:OWN + 8 - lo]


def pack_body(*refs):
    give = refs[7]
    give[0] = jnp.zeros((120, 128), F32)
    for k in range(7):
        for l in range(NL):
            part = refs[k][l, :SLAB]
            give[k + 1, l * SLAB:(l + 1) * SLAB] = part[:, :128]
            give[k + 1, 60 + l * SLAB:60 + (l + 1) * SLAB] = part[:, 128:]


def final_body(f, got, out):
    for l in range(NL):
        for t in range(8):
            out[l, t * SLAB:(t + 1) * SLAB] = f[l, t * SLAB:(t + 1) * SLAB] + unpack(got[t], l)


def swap_on(x):
    n = lax.axis_size("space")
    return lax.ppermute(x, "space", [(i, i ^ 1) for i in range(n)])


def swap_off(x):
    n, groups = lax.axis_size("space"), lax.axis_size("tm")
    pairs = []
    for t in range(groups):
        for i in range(n):
            if i in (0, n - 1):
                pairs.append((t * n + i, (t ^ 1) * n + i))
            else:
                pairs.append((t * n + i, t * n + (i + 1 if i % 2 else i - 1)))
    return lax.ppermute(x, ("tm", "space"), pairs)


def round_x(on, off):
    got_off = swap_off(off)
    return swap_on(on), got_off


def shift_tm(x, by):
    n = lax.axis_size("tm")
    return lax.ppermute(x, "tm", [(i, (i + by) % n) for i in range(n)])


def on_device(c_points, region, cond_scale, source, plan):
    c = c_points[0]
    ids = jnp.stack([lax.axis_index("tm"), lax.axis_index("space"), lax.axis_size("space")]).astype(jnp.int32)
    own, edge, ext, pay = (NL, NY, NZ), (W, NY, NZ), (EXT, NY, NZ), (7, NY, NZ)
    cond, cap, on, off = call(
        prep_body, [own, own, pay, pay], [SM] + [VM] * 2, name="prep", limit=16)(ids, region, cond_scale)
    mat_on, mat_off = round_x(on, off)
    on, off = call(state_body, [pay, pay], [SM, HB, HB], [pltpu.SemaphoreType.DMA((4,))], name="state")(ids, c, source)
    on, off = round_x(on, off)
    c_next = shift_tm(c, -1)
    fx, fy, fz, inv, capx, coef = call(
        coef_body, [ext] * 5 + [(5, EXT, HR, NZ)], [SM] + [VM] * 4, [pltpu.VMEM(ext, F32)] * 2, name="coef",
        flops=10_000_000)(ids, cond, cap, mat_on, mat_off)
    src_on, src_off = on, off
    u, fine = c, []
    for j in range(4):
        if j > 0:
            on, off = round_x(on, off)
        early = call(functools.partial(early_body, j), [ext] * 4 + [(NY, NZ)], [SM, SM] + [VM] * 9, name="early",
                     flops=15_000_000, limit=16)(ids, plan, u, on, source, src_on, fx, fy, fz, inv, capx)
        args = (ids, plan, u, off, source, src_off, fx, fy, fz, inv, capx, *early)
        if j < 3:
            u, on, off = call(functools.partial(late_body, j), [own, edge, edge], [SM, SM] + [VM] * 14,
                              [pltpu.VMEM(ext, F32)] * 4, name="late", flops=15_000_000, limit=16)(*args)
        else:
            u, give = call(functools.partial(late_body, j), [own, (8, 120, 128)], [SM, SM] + [VM] * 15,
                           [pltpu.VMEM(ext, F32)] * 4, name="late", flops=15_000_000, limit=16)(*args, c_next)
        fine.append(u)
    got = lax.all_to_all(give, "tm", 0, 0, tiled=True)
    fwd, bwd = call(ypay_body, [(NL, 32, NZ)] * 2, [VM], name="ypay")(got)
    low, high = shift_tm(fwd, 1), shift_tm(bwd, -1)
    slab, side = (NL, HR, NZ), (W, HR, NZ)
    dx, on, off = call(ymerge_body, [(7,) + slab, side, side], [SM] + [VM] * 3, name="ymerge")(ids, got, low, high)
    e = dx[0]
    parts = []
    for k in range(1, 8):
        on, off = round_x(on, off)
        kind = "last" if k == 7 else "y" if k in (3, 5) else "x"
        body = functools.partial(stage_body, k, kind)
        lo, hi = WINDOWS[k]
        small = [pltpu.VMEM((EXT, hi - lo, NZ), F32)] * 3
        if kind == "last":
            (a,) = call(body, [(NL, 16, NZ)], [SM] + [VM] * 4, small, name="stage", limit=16)(ids, coef, e, on, off)
        else:
            lo, hi = WINDOWS[k + 1]
            side = (W, hi - lo, NZ)
            ends = (NL, 8, NZ) if kind == "y" else side
            a, e, p, q = call(body, [(NL, 16, NZ), slab, ends, ends], [SM] + [VM] * 5, small, name="stage", limit=16)(
                ids, coef, e, on, off, dx)
            if kind == "y":
                low, high = shift_tm(p, 1), shift_tm(q, -1)
                e, on, off = call(merge_body, [slab, side, side], [SM] + [VM] * 3, name="merge")(ids, e, low, high)
            else:
                on, off = p, q
        parts.append(a)
    (give,) = call(pack_body, [(8, 120, 128)], [VM] * 7, name="pack", limit=16)(*parts)
    back = lax.all_to_all(give, "tm", 0, 0, tiled=True)
    (corrected,) = call(final_body, [own], [VM] * 2, name="final")(u, back)
    return jnp.stack(fine), corrected[None]


def solution(mesh):
    in_specs = (
        P("tm", "space", None, None),
        P("space", None, None),
        P("space", None, None),
        P("space", None, None),
        P("tm"),
    )
    out_specs = (P("tm", "space", None, None), P("tm", "space", None, None))
    return jax.shard_map(
        on_device, mesh=mesh, in_specs=in_specs, out_specs=out_specs, check_vma=False
    )
```

```python
import functools
import jax
import jax.numpy as jnp
from jax import lax
from jax.experimental import pallas as pl
from jax.experimental.pallas import tpu as pltpu
from jax.sharding import PartitionSpec as P

F32 = jnp.float32
VM = pl.BlockSpec(memory_space=pltpu.VMEM)
SM = pl.BlockSpec(memory_space=pltpu.SMEM)
HB = pl.BlockSpec(memory_space=pltpu.MemorySpace.HBM)
NY, NZ = 96, 256
NL = 5
W = 4
SWEEPS = 4
EXT = NL + 2 * W
SLAB = 12
HR = 40
OWN = 16


def call(body, outs, ins, scratch=(), name=None, flops=0, limit=40):
    return pl.pallas_call(
        body,
        out_shape=[jax.ShapeDtypeStruct(s, F32) for s in outs],
        in_specs=ins,
        out_specs=[VM] * len(outs),
        scratch_shapes=list(scratch),
        compiler_params=pltpu.CompilerParams(vmem_limit_bytes=limit * 2**20),
        cost_estimate=pl.CostEstimate(flops=flops, bytes_accessed=4_000_000, transcendentals=0),
        name=name,
    )


def up_roll(x, axis):
    return pltpu.roll(x, x.shape[axis] - 1, axis)


def down_roll(x, axis):
    return pltpu.roll(x, 1, axis)


def place_halo(par, dst, on, off, first, count):
    @pl.when(par == 0)
    def _():
        dst[W - count:W] = off[first:first + count]
        dst[W + NL:W + NL + count] = on[first:first + count]

    @pl.when(par == 1)
    def _():
        dst[W - count:W] = on[first:first + count]
        dst[W + NL:W + NL + count] = off[first:first + count]


def give_edges(par, src, on, off, first, count, lo=0, hi=None):
    hi = src.shape[1] if hi is None else hi

    @pl.when(par == 0)
    def _():
        on[first:first + count] = src[NL - count:NL, lo:hi]
        off[first:first + count] = src[0:count, lo:hi]

    @pl.when(par == 1)
    def _():
        on[first:first + count] = src[0:count, lo:hi]
        off[first:first + count] = src[NL - count:NL, lo:hi]


def put_edge(par, on, off, i, v):
    low, high = (off, on) if par == 0 else (on, off)
    if i < W:
        low[i] = v
    if i >= NL - W:
        high[i - (NL - W)] = v


def prep_body(ids, region, scale, cond, cap, on, off):
    par = ids[1] % 2
    for l in range(NL):
        kind = region[l]
        cap[l] = jnp.where(kind == 0, 2.0, jnp.where(kind == 1, 1.2, 1.6)).astype(F32)
        cond[l] = jnp.where(kind == 0, 0.3, jnp.where(kind == 1, 4.0, 2.5)).astype(F32) * scale[l]
    give_edges(par, cond, on, off, 0, 4)
    give_edges(par, cap, on, off, 4, 3)


def state_body(ids, c, source, on, off, sems):
    par = ids[1] % 2
    copies = [pltpu.make_async_copy(src, dst, sems.at[n]) for n, (src, dst) in enumerate([
        (c.at[pl.ds(1 - par, 4)], on.at[0:4]),
        (c.at[pl.ds(par, 4)], off.at[0:4]),
        (source.at[pl.ds(2 - 2 * par, 3)], on.at[4:7]),
        (source.at[pl.ds(2 * par, 3)], off.at[4:7]),
    ])]
    for copy in copies:
        copy.start()
    for copy in copies:
        copy.wait()


def coef_body(ids, cond, cap, on, off, fx, fy, fz, inv, capx, slabs, invc, condx):
    sp = ids[1]
    par = sp % 2
    condx[W:W + NL] = cond[...]
    capx[W:W + NL] = cap[...]
    place_halo(par, condx, on, off, 0, 4)
    place_halo(par, capx, on, off, 4, 3)
    zero = jnp.zeros((W, NY, NZ), F32)

    @pl.when(sp == 0)
    def _():
        condx[0:W] = zero

    @pl.when(sp == ids[2] - 1)
    def _():
        condx[W + NL:EXT] = zero

    rows = lax.broadcasted_iota(jnp.int32, (NY, NZ), 0)
    lanes = lax.broadcasted_iota(jnp.int32, (NY, NZ), 1)
    for l in range(1, EXT - 1):
        k = condx[l]
        f0 = 0.5 * (k + condx[l - 1])
        f1 = 0.5 * (k + condx[l + 1])
        f2 = 0.5 * (k + jnp.where(rows == 0, 0.0, down_roll(k, 0)))
        f3 = 0.5 * (k + jnp.where(rows == NY - 1, 0.0, up_roll(k, 0)))
        f4 = 0.5 * (k + jnp.where(lanes == 0, 0.0, down_roll(k, 1)))
        f5 = 0.5 * (k + jnp.where(lanes == NZ - 1, 0.0, up_roll(k, 1)))
        total = ((((f0 + f1) + f2) + f3) + f4) + f5
        heat = capx[l]
        fx[l] = f0
        fy[l] = jnp.where(rows == 0, 0.0, f2)
        fz[l] = jnp.where(lanes == 0, 0.0, f4)
        inv[l] = 1.0 / (heat * 4.0 + total)
        invc[l] = 1.0 / (heat + total)
    fx[EXT - 1] = 0.5 * (condx[EXT - 1] + condx[EXT - 2])

    @pl.when(sp == 0)
    def _():
        fx[W] = jnp.zeros((NY, NZ), F32)

    @pl.when(sp == ids[2] - 1)
    def _():
        fx[W + NL] = jnp.zeros((NY, NZ), F32)

    shift = (16 + 128 - 12 * ids[0]) % 128
    spare = jnp.zeros((128 - NY, NZ), F32)
    for n, ref in enumerate((fx, fy, fz, invc, capx)):
        for l in range(1, EXT if n == 0 else EXT - 1):
            v = jnp.concatenate([ref[l], spare], axis=0)
            slabs[n, l] = pltpu.roll(v, shift, 0)[:HR]


EARLY = (((5, 11), (6, 10), (7, 9), (8, 8)), ((1, 7), (2, 6), (3, 5), (4, 4)))
LATE = (((1, 4), (2, 5), (3, 6), (4, 7)), ((8, 11), (7, 10), (6, 9), (5, 8)))


def fine_part(par, late, amp, u_old, got, source, src_got, fx, fy, fz, inv, capx, early, mine, store):
    spans = (LATE if late else EARLY)[par]
    high = (par == 0) != late
    start = W + NL if high else 0

    def has(n, l):
        return spans[n][0] <= l <= spans[n][1]

    def start_value(l):
        return u_old[l - W] if W <= l < W + NL else got[l - start]

    def heat(l):
        return source[l - W] if W <= l < W + NL else src_got[4 + l - (start if high else 1)]

    def value(n, l):
        if n == 0:
            return start_value(l)
        return (mine if has(n - 1, l) else early)[n][l]

    for n in range(SWEEPS):
        for l in range(spans[n][0], spans[n][1] + 1):
            if n == 0:
                rhs = capx[l] * 4.0 * start_value(l) + amp * heat(l)
                mine[0][l] = rhs
            else:
                rhs = (mine if has(0, l) else early)[0][l]
            w = value(n, l)
            a = fy[l]
            b = fz[l]
            total = rhs + fx[l] * value(n, l - 1) + fx[l + 1] * value(n, l + 1)
            total = total + a * down_roll(w, 0) + up_roll(a * w, 0)
            total = total + b * down_roll(w, 1) + up_roll(b * w, 1)
            v = total * inv[l]
            if n == SWEEPS - 1:
                store(l, v)
            else:
                mine[n + 1][l] = v


def early_body(j, ids, plan, u_old, got, source, src_got, fx, fy, fz, inv, capx, beta, w1, w2, w3, last):
    amp = plan[j].astype(F32) * 0.5
    mine = (beta, w1, w2, w3)

    def store(l, v):
        last[...] = v
    for par in (0, 1):
        @pl.when(ids[1] % 2 == par)
        def _():
            fine_part(par, False, amp, u_old, got, source, src_got, fx, fy, fz, inv, capx, mine, mine, store)


def late_body(j, ids, plan, u_old, got, source, src_got, fx, fy, fz, inv, capx, beta, w1, w2, w3, last, *rest):
    amp = plan[j].astype(F32) * 0.5
    if j == 3:
        c_next, u, give, *mine = rest
    else:
        u, son, soff, *mine = rest

    def store(par, l, v):
        u[l - W] = v
        if j < 3:
            put_edge(par, son, soff, l - W, v)
    for par in (0, 1):
        @pl.when(ids[1] % 2 == par)
        def _():
            fine_part(par, True, amp, u_old, got, source, src_got, fx, fy, fz, inv, capx, (beta, w1, w2, w3), mine,
                      functools.partial(store, par))
            store(par, W + NL - 1 if par == 0 else W, last[...])
    if j < 3:
        return
    for l in range(NL):
        d = u[l] - c_next[l]
        for t in range(8):
            part = d[t * SLAB:(t + 1) * SLAB]
            give[t, l * SLAB:(l + 1) * SLAB] = part[:, :128]
            give[t, 60 + l * SLAB:60 + (l + 1) * SLAB] = part[:, 128:]


def unpack(chunk, l):
    return jnp.concatenate([chunk[l * SLAB:(l + 1) * SLAB], chunk[60 + l * SLAB:60 + (l + 1) * SLAB]], axis=1)


DEPTHS = ((1, 12, 0), (2, 8, 12), (3, 4, 20), (5, 4, 24), (7, 4, 28))


def ypay_body(got, fwd, bwd):
    for l in range(NL):
        for k, deep, at in DEPTHS:
            v = unpack(got[k - 1], l)
            fwd[l, at:at + deep] = v[SLAB - deep:]
            bwd[l, at:at + deep] = v[:deep]


def ymerge_body(ids, got, low, high, dx, on, off):
    dx[...] = jnp.zeros((7, NL, HR, NZ), F32)
    halo = {k: (deep, at) for k, deep, at in DEPTHS}
    for l in range(NL):
        for k in range(1, 8):
            dx[k - 1, l, OWN:OWN + SLAB] = unpack(got[k - 1], l)
            if k in halo:
                deep, at = halo[k]
                dx[k - 1, l, OWN - deep:OWN] = low[l, at:at + deep]
                dx[k - 1, l, OWN + SLAB:OWN + SLAB + deep] = high[l, at:at + deep]
    give_edges(ids[1] % 2, dx.at[0], on, off, 0, 4)


def merge_body(ids, e, low, high, ex, on, off):
    ex[...] = e[...]
    ex[:, OWN - 8:OWN] = low[...]
    ex[:, OWN + SLAB:OWN + SLAB + 8] = high[...]
    give_edges(ids[1] % 2, ex, on, off, 0, 4, *WINDOWS[4])


WINDOWS = {1: (0, 40), 2: (8, 40), 3: (8, 32), 4: (8, 40), 5: (8, 32), 6: (8, 40), 7: (8, 32)}


def stage_body(k, kind, ids, *refs):
    for par in (0, 1):
        @pl.when(ids[1] % 2 == par)
        def _():
            stage_part(k, kind, par, *refs)


def stage_part(k, kind, par, coef, e, on, off, *rest):
    lo, hi = WINDOWS[k]
    if kind == "last":
        packed, give, wa, wb, beta = rest
        give[0:7] = packed[0:7]
    else:
        dx, a, nxt, p, q, wa, wb, beta = rest
    low, high = (off, on) if par == 0 else (on, off)
    fx, fy, fz, inv, cap = [functools.partial(lambda n, l: coef[n, l, lo:hi], n) for n in range(5)]

    def start_value(l):
        if W <= l < W + NL:
            return e[l - W, lo:hi]
        return low[l] if l < W else high[l - W - NL]

    for n, (src, dst) in enumerate(((start_value, wb), (wb, wa), (wa, wb), (wb, None))):
        for l in range(n + 1, EXT - 1 - n):
            if n == 0:
                w, left, right = src(l), src(l - 1), src(l + 1)
                rhs = cap(l) * w
                beta[l] = rhs
            else:
                w, left, right = src[l], src[l - 1], src[l + 1]
                rhs = beta[l]
            f, g = fy(l), fz(l)
            total = rhs + fx(l) * left + fx(l + 1) * right
            total = total + f * down_roll(w, 0) + up_roll(f * w, 0)
            total = total + g * down_roll(w, 1) + up_roll(g * w, 1)
            v = total * inv(l)
            if dst is not None:
                dst[l] = v
                continue
            i = l - W
            if kind == "last":
                part = v[OWN - lo:OWN - lo + SLAB]
                give[7, i * SLAB:(i + 1) * SLAB] = part[:, :128]
                give[7, 60 + i * SLAB:60 + (i + 1) * SLAB] = part[:, 128:]
                continue
            a[i] = v[OWN - lo:OWN - lo + 16]
            v = v + dx[k, i, lo:hi]
            nxt[i, lo:hi] = v
            if kind == "x":
                at, end = WINDOWS[k + 1]
                put_edge(par, p, q, i, v[at - lo:end - lo])
            else:
                nxt[i, :lo] = jnp.zeros((lo, NZ), F32)
                nxt[i, hi:] = jnp.zeros((HR - hi, NZ), F32)
                p[i] = v[OWN + SLAB - 8 - lo:OWN + SLAB - lo]
                q[i] = v[OWN - lo:OWN + 8 - lo]


def put_chunk(chunk, own):
    for l in range(NL):
        part = own(l)
        chunk[l * SLAB:(l + 1) * SLAB] = part[:, :128]
        chunk[60 + l * SLAB:60 + (l + 1) * SLAB] = part[:, 128:]


def pack_body(*refs):
    give = refs[6]
    give[0] = jnp.zeros((120, 128), F32)
    for k in range(6):
        put_chunk(give.at[k + 1], lambda l: refs[k][l, :SLAB])


def final_body(f, got, out):
    for l in range(NL):
        for t in range(8):
            out[l, t * SLAB:(t + 1) * SLAB] = f[l, t * SLAB:(t + 1) * SLAB] + unpack(got[t], l)


def swap_on(x):
    n = lax.axis_size("space")
    return lax.ppermute(x, "space", [(i, i ^ 1) for i in range(n)])


def swap_off(x):
    n, groups = lax.axis_size("space"), lax.axis_size("tm")
    pairs = []
    for t in range(groups):
        for i in range(n):
            if i in (0, n - 1):
                pairs.append((t * n + i, (t ^ 1) * n + i))
            else:
                pairs.append((t * n + i, t * n + (i + 1 if i % 2 else i - 1)))
    return lax.ppermute(x, ("tm", "space"), pairs)


def round_x(on, off):
    got_off = swap_off(off)
    return swap_on(on), got_off


def shift_tm(x, by):
    n = lax.axis_size("tm")
    return lax.ppermute(x, "tm", [(i, (i + by) % n) for i in range(n)])


def on_device(c_points, region, cond_scale, source, plan):
    c = c_points[0]
    ids = jnp.stack([lax.axis_index("tm"), lax.axis_index("space"), lax.axis_size("space")]).astype(jnp.int32)
    own, edge, ext, pay = (NL, NY, NZ), (W, NY, NZ), (EXT, NY, NZ), (7, NY, NZ)
    cond, cap, on, off = call(
        prep_body, [own, own, pay, pay], [SM] + [VM] * 2, name="prep", limit=16)(ids, region, cond_scale)
    mat_on, mat_off = round_x(on, off)
    on, off = call(state_body, [pay, pay], [SM, HB, HB], [pltpu.SemaphoreType.DMA((4,))], name="state")(ids, c, source)
    on, off = round_x(on, off)
    c_next = shift_tm(c, -1)
    fx, fy, fz, inv, capx, coef = call(
        coef_body, [ext] * 5 + [(5, EXT, HR, NZ)], [SM] + [VM] * 4, [pltpu.VMEM(ext, F32)] * 2, name="coef",
        flops=10_000_000)(ids, cond, cap, mat_on, mat_off)
    src_on, src_off = on, off
    u, fine = c, []
    for j in range(4):
        if j > 0:
            on, off = round_x(on, off)
        early = call(functools.partial(early_body, j), [ext] * 4 + [(NY, NZ)], [SM, SM] + [VM] * 9, name="early",
                     flops=15_000_000, limit=16)(ids, plan, u, on, source, src_on, fx, fy, fz, inv, capx)
        args = (ids, plan, u, off, source, src_off, fx, fy, fz, inv, capx, *early)
        if j < 3:
            u, on, off = call(functools.partial(late_body, j), [own, edge, edge], [SM, SM] + [VM] * 14,
                              [pltpu.VMEM(ext, F32)] * 4, name="late", flops=15_000_000, limit=16)(*args)
        else:
            u, give = call(functools.partial(late_body, j), [own, (8, 120, 128)], [SM, SM] + [VM] * 15,
                           [pltpu.VMEM(ext, F32)] * 4, name="late", flops=15_000_000, limit=16)(*args, c_next)
        fine.append(u)
    got = lax.all_to_all(give, "tm", 0, 0, tiled=True)
    fwd, bwd = call(ypay_body, [(NL, 32, NZ)] * 2, [VM], name="ypay")(got)
    low, high = shift_tm(fwd, 1), shift_tm(bwd, -1)
    slab, side = (NL, HR, NZ), (W, HR, NZ)
    dx, on, off = call(ymerge_body, [(7,) + slab, side, side], [SM] + [VM] * 3, name="ymerge")(ids, got, low, high)
    e = dx[0]
    parts = []
    for k in range(1, 8):
        on, off = round_x(on, off)
        kind = "last" if k == 7 else "y" if k in (3, 5) else "x"
        body = functools.partial(stage_body, k, kind)
        lo, hi = WINDOWS[k]
        small = [pltpu.VMEM((EXT, hi - lo, NZ), F32)] * 3
        if kind == "last":
            (give,) = call(pack_body, [(8, 120, 128)], [VM] * 6, name="pack", limit=16)(*parts)
            (give,) = call(body, [(8, 120, 128)], [SM] + [VM] * 5, small, name="stage", limit=16)(
                ids, coef, e, on, off, give)
            break
        else:
            lo, hi = WINDOWS[k + 1]
            side = (W, hi - lo, NZ)
            ends = (NL, 8, NZ) if kind == "y" else side
            a, e, p, q = call(body, [(NL, 16, NZ), slab, ends, ends], [SM] + [VM] * 5, small, name="stage", limit=16)(
                ids, coef, e, on, off, dx)
            if kind == "y":
                low, high = shift_tm(p, 1), shift_tm(q, -1)
                e, on, off = call(merge_body, [slab, side, side], [SM] + [VM] * 3, name="merge")(ids, e, low, high)
            else:
                on, off = p, q
        parts.append(a)
    back = lax.all_to_all(give, "tm", 0, 0, tiled=True)
    (corrected,) = call(final_body, [own], [VM] * 2, name="final")(u, back)
    return jnp.stack(fine), corrected[None]


def solution(mesh):
    in_specs = (
        P("tm", "space", None, None),
        P("space", None, None),
        P("space", None, None),
        P("space", None, None),
        P("tm"),
    )
    out_specs = (P("tm", "space", None, None), P("tm", "space", None, None))
    return jax.shard_map(
        on_device, mesh=mesh, in_specs=in_specs, out_specs=out_specs, check_vma=False
    )
```

```python
import functools
import jax
import jax.numpy as jnp
from jax import lax
from jax.experimental import pallas as pl
from jax.experimental.pallas import tpu as pltpu
from jax.sharding import PartitionSpec as P

F32 = jnp.float32
VM = pl.BlockSpec(memory_space=pltpu.VMEM)
SM = pl.BlockSpec(memory_space=pltpu.SMEM)
HB = pl.BlockSpec(memory_space=pltpu.MemorySpace.HBM)
NY, NZ = 96, 256
NL = 5
W = 4
SWEEPS = 4
EXT = NL + 2 * W
SLAB = 12
HR = 40
OWN = 16


def call(body, outs, ins, scratch=(), name=None, flops=0, limit=40):
    return pl.pallas_call(
        body,
        out_shape=[jax.ShapeDtypeStruct(s, F32) for s in outs],
        in_specs=ins,
        out_specs=[VM] * len(outs),
        scratch_shapes=list(scratch),
        compiler_params=pltpu.CompilerParams(vmem_limit_bytes=limit * 2**20),
        cost_estimate=pl.CostEstimate(flops=flops, bytes_accessed=4_000_000, transcendentals=0),
        name=name,
    )


def up_roll(x, axis):
    return pltpu.roll(x, x.shape[axis] - 1, axis)


def down_roll(x, axis):
    return pltpu.roll(x, 1, axis)


def place_halo(par, dst, on, off, first, count):
    @pl.when(par == 0)
    def _():
        dst[W - count:W] = off[first:first + count]
        dst[W + NL:W + NL + count] = on[first:first + count]

    @pl.when(par == 1)
    def _():
        dst[W - count:W] = on[first:first + count]
        dst[W + NL:W + NL + count] = off[first:first + count]


def give_edges(par, src, on, off, first, count, lo=0, hi=None):
    hi = src.shape[1] if hi is None else hi

    @pl.when(par == 0)
    def _():
        on[first:first + count] = src[NL - count:NL, lo:hi]
        off[first:first + count] = src[0:count, lo:hi]

    @pl.when(par == 1)
    def _():
        on[first:first + count] = src[0:count, lo:hi]
        off[first:first + count] = src[NL - count:NL, lo:hi]


def put_edge(par, on, off, i, v):
    low, high = (off, on) if par == 0 else (on, off)
    if i < W:
        low[i] = v
    if i >= NL - W:
        high[i - (NL - W)] = v


def prep_body(ids, region, scale, cond, cap, on, off):
    par = ids[1] % 2
    for l in range(NL):
        kind = region[l]
        cap[l] = jnp.where(kind == 0, 2.0, jnp.where(kind == 1, 1.2, 1.6)).astype(F32)
        cond[l] = jnp.where(kind == 0, 0.3, jnp.where(kind == 1, 4.0, 2.5)).astype(F32) * scale[l]
    give_edges(par, cond, on, off, 0, 4)
    give_edges(par, cap, on, off, 4, 3)


def state_body(ids, c, source, on, off, sems):
    par = ids[1] % 2
    copies = [pltpu.make_async_copy(src, dst, sems.at[n]) for n, (src, dst) in enumerate([
        (c.at[pl.ds(1 - par, 4)], on.at[0:4]),
        (c.at[pl.ds(par, 4)], off.at[0:4]),
        (source.at[pl.ds(2 - 2 * par, 3)], on.at[4:7]),
        (source.at[pl.ds(2 * par, 3)], off.at[4:7]),
    ])]
    for copy in copies:
        copy.start()
    for copy in copies:
        copy.wait()


def coef_body(ids, cond, cap, on, off, fx, fy, fz, inv, capx, slabs, invc, condx):
    sp = ids[1]
    par = sp % 2
    condx[W:W + NL] = cond[...]
    capx[W:W + NL] = cap[...]
    place_halo(par, condx, on, off, 0, 4)
    place_halo(par, capx, on, off, 4, 3)
    zero = jnp.zeros((W, NY, NZ), F32)

    @pl.when(sp == 0)
    def _():
        condx[0:W] = zero

    @pl.when(sp == ids[2] - 1)
    def _():
        condx[W + NL:EXT] = zero

    rows = lax.broadcasted_iota(jnp.int32, (NY, NZ), 0)
    lanes = lax.broadcasted_iota(jnp.int32, (NY, NZ), 1)
    for l in range(1, EXT - 1):
        k = condx[l]
        f0 = 0.5 * (k + condx[l - 1])
        f1 = 0.5 * (k + condx[l + 1])
        f2 = 0.5 * (k + jnp.where(rows == 0, 0.0, down_roll(k, 0)))
        f3 = 0.5 * (k + jnp.where(rows == NY - 1, 0.0, up_roll(k, 0)))
        f4 = 0.5 * (k + jnp.where(lanes == 0, 0.0, down_roll(k, 1)))
        f5 = 0.5 * (k + jnp.where(lanes == NZ - 1, 0.0, up_roll(k, 1)))
        total = ((((f0 + f1) + f2) + f3) + f4) + f5
        heat = capx[l]
        fx[l] = f0
        fy[l] = jnp.where(rows == 0, 0.0, f2)
        fz[l] = jnp.where(lanes == 0, 0.0, f4)
        inv[l] = 1.0 / (heat * 4.0 + total)
        invc[l] = 1.0 / (heat + total)
    fx[EXT - 1] = 0.5 * (condx[EXT - 1] + condx[EXT - 2])

    @pl.when(sp == 0)
    def _():
        fx[W] = jnp.zeros((NY, NZ), F32)

    @pl.when(sp == ids[2] - 1)
    def _():
        fx[W + NL] = jnp.zeros((NY, NZ), F32)

    shift = (16 + 128 - 12 * ids[0]) % 128
    spare = jnp.zeros((128 - NY, NZ), F32)
    for n, ref in enumerate((fx, fy, fz, invc, capx)):
        for l in range(1, EXT if n == 0 else EXT - 1):
            v = jnp.concatenate([ref[l], spare], axis=0)
            slabs[n, l] = pltpu.roll(v, shift, 0)[:HR]


EARLY = (((5, 11), (6, 10), (7, 9), (8, 8)), ((1, 7), (2, 6), (3, 5), (4, 4)))
LATE = (((1, 4), (2, 5), (3, 6), (4, 7)), ((8, 11), (7, 10), (6, 9), (5, 8)))


def fine_part(par, late, amp, u_old, got, source, src_got, fx, fy, fz, inv, capx, early, mine, store):
    spans = (LATE if late else EARLY)[par]
    high = (par == 0) != late
    start = W + NL if high else 0

    def has(n, l):
        return spans[n][0] <= l <= spans[n][1]

    def start_value(l):
        return u_old[l - W] if W <= l < W + NL else got[l - start]

    def heat(l):
        return source[l - W] if W <= l < W + NL else src_got[4 + l - (start if high else 1)]

    def value(n, l):
        if n == 0:
            return start_value(l)
        return (mine if has(n - 1, l) else early)[n][l]

    for n in range(SWEEPS):
        for l in range(spans[n][0], spans[n][1] + 1):
            if n == 0:
                rhs = capx[l] * 4.0 * start_value(l) + amp * heat(l)
                mine[0][l] = rhs
            else:
                rhs = (mine if has(0, l) else early)[0][l]
            w = value(n, l)
            a = fy[l]
            b = fz[l]
            total = rhs + fx[l] * value(n, l - 1) + fx[l + 1] * value(n, l + 1)
            total = total + a * down_roll(w, 0) + up_roll(a * w, 0)
            total = total + b * down_roll(w, 1) + up_roll(b * w, 1)
            v = total * inv[l]
            if n == SWEEPS - 1:
                store(l, v)
            else:
                mine[n + 1][l] = v


def early_body(j, ids, plan, u_old, got, source, src_got, fx, fy, fz, inv, capx, beta, w1, w2, w3, last):
    amp = plan[j].astype(F32) * 0.5
    mine = (beta, w1, w2, w3)

    def store(l, v):
        last[...] = v
    for par in (0, 1):
        @pl.when(ids[1] % 2 == par)
        def _():
            fine_part(par, False, amp, u_old, got, source, src_got, fx, fy, fz, inv, capx, mine, mine, store)


def late_body(j, ids, plan, u_old, got, source, src_got, fx, fy, fz, inv, capx, beta, w1, w2, w3, last, *rest):
    amp = plan[j].astype(F32) * 0.5
    if j == 3:
        c_next, u, give, *mine = rest
    else:
        u, son, soff, *mine = rest

    def store(par, l, v):
        u[l - W] = v
        if j < 3:
            put_edge(par, son, soff, l - W, v)
    for par in (0, 1):
        @pl.when(ids[1] % 2 == par)
        def _():
            fine_part(par, True, amp, u_old, got, source, src_got, fx, fy, fz, inv, capx, (beta, w1, w2, w3), mine,
                      functools.partial(store, par))
            store(par, W + NL - 1 if par == 0 else W, last[...])
    if j < 3:
        return
    for l in range(NL):
        d = u[l] - c_next[l]
        for t in range(8):
            part = d[t * SLAB:(t + 1) * SLAB]
            give[t, l * SLAB:(l + 1) * SLAB] = part[:, :128]
            give[t, 60 + l * SLAB:60 + (l + 1) * SLAB] = part[:, 128:]


def unpack(chunk, l):
    return jnp.concatenate([chunk[l * SLAB:(l + 1) * SLAB], chunk[60 + l * SLAB:60 + (l + 1) * SLAB]], axis=1)


DEPTHS = ((1, 12, 0), (2, 8, 12), (3, 4, 20), (5, 4, 24), (7, 4, 28))


def ypay_body(got, fwd, bwd):
    for l in range(NL):
        for k, deep, at in DEPTHS:
            v = unpack(got[k - 1], l)
            fwd[l, at:at + deep] = v[SLAB - deep:]
            bwd[l, at:at + deep] = v[:deep]


HALOS = {k: (deep, at) for k, deep, at in DEPTHS}


def put_defect(k, l, out, got, low, high):
    deep, at = HALOS.get(k, (0, 0))
    out[:OWN - deep] = jnp.zeros((OWN - deep, NZ), F32)
    out[OWN:OWN + SLAB] = unpack(got[k - 1], l)
    if deep:
        out[OWN - deep:OWN] = low[l, at:at + deep]
        out[OWN + SLAB:OWN + SLAB + deep] = high[l, at:at + deep]
    if OWN + SLAB + deep < HR:
        out[OWN + SLAB + deep:] = jnp.zeros((HR - OWN - SLAB - deep, NZ), F32)


def ymerge_body(ids, got, low, high, e, on, off):
    for l in range(NL):
        put_defect(1, l, e.at[l], got, low, high)
    give_edges(ids[1] % 2, e, on, off, 0, 4)


def defects_body(got, low, high, dx):
    for k in range(2, 8):
        for l in range(NL):
            put_defect(k, l, dx.at[k - 1, l], got, low, high)


def merge_body(ids, e, low, high, ex, on, off):
    ex[...] = e[...]
    ex[:, OWN - 8:OWN] = low[...]
    ex[:, OWN + SLAB:OWN + SLAB + 8] = high[...]
    give_edges(ids[1] % 2, ex, on, off, 0, 4, *WINDOWS[4])


WINDOWS = {1: (0, 40), 2: (8, 40), 3: (8, 32), 4: (8, 40), 5: (8, 32), 6: (8, 40), 7: (8, 32)}


def stage_body(k, kind, ids, *refs):
    for par in (0, 1):
        @pl.when(ids[1] % 2 == par)
        def _():
            stage_part(k, kind, par, *refs)


def stage_part(k, kind, par, coef, e, on, off, *rest):
    lo, hi = WINDOWS[k]
    if kind == "last":
        packed, give, wa, wb, beta = rest
        give[0:7] = packed[0:7]
    else:
        dx, a, nxt, p, q, wa, wb, beta = rest
    low, high = (off, on) if par == 0 else (on, off)
    fx, fy, fz, inv, cap = [functools.partial(lambda n, l: coef[n, l, lo:hi], n) for n in range(5)]

    def start_value(l):
        if W <= l < W + NL:
            return e[l - W, lo:hi]
        return low[l] if l < W else high[l - W - NL]

    for n, (src, dst) in enumerate(((start_value, wb), (wb, wa), (wa, wb), (wb, None))):
        for l in range(n + 1, EXT - 1 - n):
            if n == 0:
                w, left, right = src(l), src(l - 1), src(l + 1)
                rhs = cap(l) * w
                beta[l] = rhs
            else:
                w, left, right = src[l], src[l - 1], src[l + 1]
                rhs = beta[l]
            f, g = fy(l), fz(l)
            total = rhs + fx(l) * left + fx(l + 1) * right
            total = total + f * down_roll(w, 0) + up_roll(f * w, 0)
            total = total + g * down_roll(w, 1) + up_roll(g * w, 1)
            v = total * inv(l)
            if dst is not None:
                dst[l] = v
                continue
            i = l - W
            if kind == "last":
                part = v[OWN - lo:OWN - lo + SLAB]
                give[7, i * SLAB:(i + 1) * SLAB] = part[:, :128]
                give[7, 60 + i * SLAB:60 + (i + 1) * SLAB] = part[:, 128:]
                continue
            a[i] = v[OWN - lo:OWN - lo + 16]
            v = v + dx[k, i, lo:hi]
            nxt[i, lo:hi] = v
            if kind == "x":
                at, end = WINDOWS[k + 1]
                put_edge(par, p, q, i, v[at - lo:end - lo])
            else:
                nxt[i, :lo] = jnp.zeros((lo, NZ), F32)
                nxt[i, hi:] = jnp.zeros((HR - hi, NZ), F32)
                p[i] = v[OWN + SLAB - 8 - lo:OWN + SLAB - lo]
                q[i] = v[OWN - lo:OWN + 8 - lo]


def put_chunk(chunk, own):
    for l in range(NL):
        part = own(l)
        chunk[l * SLAB:(l + 1) * SLAB] = part[:, :128]
        chunk[60 + l * SLAB:60 + (l + 1) * SLAB] = part[:, 128:]


def pack_body(*refs):
    give = refs[6]
    give[0] = jnp.zeros((120, 128), F32)
    for k in range(6):
        put_chunk(give.at[k + 1], lambda l: refs[k][l, :SLAB])


def final_body(f, got, out):
    for l in range(NL):
        for t in range(8):
            out[l, t * SLAB:(t + 1) * SLAB] = f[l, t * SLAB:(t + 1) * SLAB] + unpack(got[t], l)


def swap_on(x):
    n = lax.axis_size("space")
    return lax.ppermute(x, "space", [(i, i ^ 1) for i in range(n)])


def swap_off(x):
    n, groups = lax.axis_size("space"), lax.axis_size("tm")
    pairs = []
    for t in range(groups):
        for i in range(n):
            if i in (0, n - 1):
                pairs.append((t * n + i, (t ^ 1) * n + i))
            else:
                pairs.append((t * n + i, t * n + (i + 1 if i % 2 else i - 1)))
    return lax.ppermute(x, ("tm", "space"), pairs)


def round_x(on, off):
    got_off = swap_off(off)
    return swap_on(on), got_off


def shift_tm(x, by):
    n = lax.axis_size("tm")
    return lax.ppermute(x, "tm", [(i, (i + by) % n) for i in range(n)])


def on_device(c_points, region, cond_scale, source, plan):
    c = c_points[0]
    ids = jnp.stack([lax.axis_index("tm"), lax.axis_index("space"), lax.axis_size("space")]).astype(jnp.int32)
    own, edge, ext, pay = (NL, NY, NZ), (W, NY, NZ), (EXT, NY, NZ), (7, NY, NZ)
    cond, cap, on, off = call(
        prep_body, [own, own, pay, pay], [SM] + [VM] * 2, name="prep", limit=16)(ids, region, cond_scale)
    mat_on, mat_off = round_x(on, off)
    on, off = call(state_body, [pay, pay], [SM, HB, HB], [pltpu.SemaphoreType.DMA((4,))], name="state")(ids, c, source)
    on, off = round_x(on, off)
    c_next = shift_tm(c, -1)
    fx, fy, fz, inv, capx, coef = call(
        coef_body, [ext] * 5 + [(5, EXT, HR, NZ)], [SM] + [VM] * 4, [pltpu.VMEM(ext, F32)] * 2, name="coef",
        flops=10_000_000)(ids, cond, cap, mat_on, mat_off)
    src_on, src_off = on, off
    u, fine = c, []
    for j in range(4):
        if j > 0:
            on, off = round_x(on, off)
        early = call(functools.partial(early_body, j), [ext] * 4 + [(NY, NZ)], [SM, SM] + [VM] * 9, name="early",
                     flops=15_000_000, limit=16)(ids, plan, u, on, source, src_on, fx, fy, fz, inv, capx)
        args = (ids, plan, u, off, source, src_off, fx, fy, fz, inv, capx, *early)
        if j < 3:
            u, on, off = call(functools.partial(late_body, j), [own, edge, edge], [SM, SM] + [VM] * 14,
                              [pltpu.VMEM(ext, F32)] * 4, name="late", flops=15_000_000, limit=16)(*args)
        else:
            u, give = call(functools.partial(late_body, j), [own, (8, 120, 128)], [SM, SM] + [VM] * 15,
                           [pltpu.VMEM(ext, F32)] * 4, name="late", flops=15_000_000, limit=16)(*args, c_next)
        fine.append(u)
    got = lax.all_to_all(give, "tm", 0, 0, tiled=True)
    fwd, bwd = call(ypay_body, [(NL, 32, NZ)] * 2, [VM], name="ypay")(got)
    low, high = shift_tm(fwd, 1), shift_tm(bwd, -1)
    slab, side = (NL, HR, NZ), (W, HR, NZ)
    e, on, off = call(ymerge_body, [slab, side, side], [SM] + [VM] * 3, name="ymerge")(ids, got, low, high)
    (dx,) = call(defects_body, [(7,) + slab], [VM] * 3, name="defects")(got, low, high)
    parts = []
    for k in range(1, 8):
        on, off = round_x(on, off)
        kind = "last" if k == 7 else "y" if k in (3, 5) else "x"
        body = functools.partial(stage_body, k, kind)
        lo, hi = WINDOWS[k]
        small = [pltpu.VMEM((EXT, hi - lo, NZ), F32)] * 3
        if kind == "last":
            (give,) = call(pack_body, [(8, 120, 128)], [VM] * 6, name="pack", limit=16)(*parts)
            (give,) = call(body, [(8, 120, 128)], [SM] + [VM] * 5, small, name="stage", limit=16)(
                ids, coef, e, on, off, give)
            break
        else:
            lo, hi = WINDOWS[k + 1]
            side = (W, hi - lo, NZ)
            ends = (NL, 8, NZ) if kind == "y" else side
            a, e, p, q = call(body, [(NL, 16, NZ), slab, ends, ends], [SM] + [VM] * 5, small, name="stage", limit=16)(
                ids, coef, e, on, off, dx)
            if kind == "y":
                low, high = shift_tm(p, 1), shift_tm(q, -1)
                e, on, off = call(merge_body, [slab, side, side], [SM] + [VM] * 3, name="merge")(ids, e, low, high)
            else:
                on, off = p, q
        parts.append(a)
    back = lax.all_to_all(give, "tm", 0, 0, tiled=True)
    (corrected,) = call(final_body, [own], [VM] * 2, name="final")(u, back)
    return jnp.stack(fine), corrected[None]


def solution(mesh):
    in_specs = (
        P("tm", "space", None, None),
        P("space", None, None),
        P("space", None, None),
        P("space", None, None),
        P("tm"),
    )
    out_specs = (P("tm", "space", None, None), P("tm", "space", None, None))
    return jax.shard_map(
        on_device, mesh=mesh, in_specs=in_specs, out_specs=out_specs, check_vma=False
    )
```
